512 devices in a mesh: pa: 32 (over x, y), pb: 16 (over z, core).
Axes of the slice: x: 4, y: 8, z: 8, core: 2. Of those that a mesh axis runs over, the one named last changes fastest.
Arguments:
- queries: bfloat16 [65536, 1024], P(('pa', 'pb')), may hold values from -900 to 900
- batch_hidden: bfloat16 [8192, 1024], P(('pa', 'pb')), may hold values from -6 to 6
- pool_hidden: bfloat16 [262144, 1024], P(('pa', 'pb')), may hold values from -6 to 6
- projection: bfloat16 [1024, 1024], replicated, may hold values from -0.1875 to 0.1875
- hard_ids: int32 [65536, 16], P(('pa', 'pb')), may hold values from 0 to 8191, as said below
- query_group: int32 [65536], P(('pa', 'pb')), may hold values from 0 to 63
- labels: int32 [65536], P(('pa', 'pb')), may hold values from 0 to 63
- group_lists: int32 [64, 64], replicated, may hold values from 0 to 511, as said below
Outputs:
- query_grad: bfloat16 [65536, 1024], P(('pa', 'pb'))
- batch_hidden_grad: bfloat16 [8192, 1024], P(('pa', 'pb'))
- pool_hidden_grad: bfloat16 [262144, 1024], P(('pa', 'pb'))
The draws below stay inside these ranges and needn't reach their ends.
Inputs may be any that keep to these rules, and one draw needn't show every extreme that they name: `hard_ids`: entry k of a query's list lies in [(k % 16) * 512, (k % 16 + 1) * 512); entries may repeat. `group_lists`: each row holds 64 different values.
All inputs are finite; a program needn't handle non-finite values.
Results may differ from the reference program's by a relative error of at most 0.017.
The reference program's roundings to bfloat16 on the way count: a program that leaves them out, or rounds other values in their place, can miss the bound.
Values may be sent and summed in bfloat16 or wider, within the bound.
A program may use at most 128 MiB of HBM per device.

```python
import math
import jax
import jax.numpy as jnp
from jax import lax

D = 1024
QD = 128
PD = 512
IB = 16
NGROUPS = 64
HN = 16
GROUP = 64
NQ = 65536
NB = 8192
NPOOL = 262144
N_PA = 32
N_PB = 16
DEVICES = 512


def draw_queries(key, part):
    key_one = jax.random.fold_in(jax.random.fold_in(key, 5), 0)
    values_raw = jnp.clip(jax.random.normal(key_one, (NQ, D), jnp.float32), -6.0, 6.0)
    return values_raw.astype(jnp.bfloat16)


def draw_hard_ids(key, part):
    key_one, key_two, key_three = jax.random.split(jax.random.fold_in(key, 11), 3)
    first = jax.random.randint(key_one, (NQ, HN), 0, PD)
    second = jax.random.randint(key_two, (NQ, HN), 0, PD)
    skewed = first * second // max(PD - 1, 1)
    shuffle = jax.random.permutation(key_three, PD)
    owner_index = jnp.arange(HN) % N_PB
    return (owner_index[None, :] * PD + jnp.take(shuffle, skewed)).astype(jnp.int32)


def draw_group_lists(key, part):
    key_list = jax.random.split(jax.random.fold_in(key, 23), NGROUPS)
    rows_all = jax.vmap(lambda one_key: jax.random.permutation(one_key, N_PA * IB)[:GROUP])(key_list)
    return rows_all.astype(jnp.int32)


def plant(entries, own_key, smallest, high):
    longest = entries.shape.index(max(entries.shape))
    spots = []
    for shift in (0, 1):
        where = [jax.random.randint(jax.random.fold_in(own_key, axis), (), 0, length) for axis, length in enumerate(entries.shape)]
        where[longest] = (where[longest] + shift) % entries.shape[longest]
        spots.append(tuple(where))
    return entries.at[spots[0]].set(smallest).at[spots[1]].set(high)


def block_scale(rng, shape, cuts, smallest, high):
    def one(dim, shards_of):
        heights = jax.random.uniform(jax.random.fold_in(jax.random.fold_in(rng, 6), dim), (shards_of,), jnp.float32, smallest / len(cuts), high / len(cuts))
        return jnp.repeat(jnp.exp(heights), shape[dim] // shards_of).reshape((-1,) + (1,) * (len(shape) - dim - 1))

    gain = one(*cuts[0])
    for cut in cuts[1:]:
        gain = gain * one(*cut)
    return gain


def bell_draw(stream_key, shape, spread, limit, cuts=(), kind=jnp.bfloat16):
    loudness = block_scale(stream_key, shape, cuts, -0.22, 0.18) if cuts else 1.0
    array = jax.random.normal(stream_key, shape, jnp.float32) * spread * loudness
    return jnp.minimum(jnp.maximum(array, -limit), limit).astype(kind)


def setup_inputs(seed: int = 0) -> dict:
    keys = jax.random.split(jax.random.key(seed), 9)
    queries = draw_queries(jax.random.fold_in(keys[8], 71), 0)
    batch_hidden = bell_draw(keys[1], (NB, D), 1.0, 6.0, ((0, 512),))
    pool_hidden = bell_draw(keys[2], (NPOOL, D), 1.0, 6.0, ((0, 512),))
    projection = bell_draw(keys[3], (D, D), D ** -0.5, 0.1875)
    hard_ids = draw_hard_ids(jax.random.fold_in(keys[8], 71), 0)
    query_group = plant(jax.random.randint(keys[5], (NQ,), 0, NGROUPS), jax.random.fold_in(keys[5], 1), 0, NGROUPS - 1).astype(jnp.int32)
    labels = plant(jax.random.randint(keys[6], (NQ,), 0, GROUP), jax.random.fold_in(keys[6], 1), 0, GROUP - 1).astype(jnp.int32)
    group_lists = draw_group_lists(jax.random.fold_in(keys[8], 71), 0)
    return {"queries": queries, "batch_hidden": batch_hidden, "pool_hidden": pool_hidden, "projection": projection, "hard_ids": hard_ids, "query_group": query_group, "labels": labels, "group_lists": group_lists}


def reference(queries, batch_hidden, pool_hidden, projection, hard_ids, query_group, labels, group_lists):
    score_scale = 1.0 / math.sqrt(D)
    batch_proj = jnp.dot(batch_hidden, projection, preferred_element_type=jnp.float32).astype(jnp.bfloat16)
    pool_proj = jnp.dot(pool_hidden, projection, preferred_element_type=jnp.float32).astype(jnp.bfloat16)
    batch_table = batch_proj.reshape(N_PA, N_PB, IB, D)
    pool_table = pool_proj.reshape(N_PA, N_PB * PD, D)
    query_blocks = queries.reshape(DEVICES, QD, D)
    hard_blocks = hard_ids.reshape(DEVICES, QD, HN)
    group_blocks = query_group.reshape(DEVICES, QD)
    label_blocks = labels.reshape(DEVICES, QD)
    positions = jnp.arange(GROUP + HN, dtype=jnp.int32)
    query_index = jnp.arange(QD, dtype=jnp.int32)

    def one_block(carry, inputs):
        batch_grad, pool_grad = carry
        device_index, query_block, hard_block, group_block, label_block = inputs
        row_index = (device_index // N_PB).astype(jnp.int32)
        col_index = (device_index % N_PB).astype(jnp.int32)
        column = lax.dynamic_index_in_dim(batch_table, col_index, 1, keepdims=False).reshape(N_PA * IB, D)
        pool_row = lax.dynamic_index_in_dim(pool_table, row_index, 0, keepdims=False)
        chosen = jnp.take(group_lists, group_block, axis=0)
        group_rows = jnp.take(column, chosen, axis=0).astype(jnp.float32)
        hard_rows = jnp.take(pool_row, hard_block, axis=0).astype(jnp.float32)
        query_wide = query_block.astype(jnp.float32)
        group_scores = score_scale * jnp.einsum('id,icd->ic', query_wide, group_rows, precision=lax.Precision.HIGHEST)
        hard_scores = score_scale * jnp.einsum('id,ikd->ik', query_wide, hard_rows, precision=lax.Precision.HIGHEST)
        scores = jnp.concatenate([group_scores, hard_scores], axis=1)
        likely = jax.nn.softmax(scores, axis=1)
        target = (positions[None, :] == label_block[:, None]).astype(jnp.float32)
        dscore = lax.optimization_barrier((likely - target).astype(jnp.bfloat16)).astype(jnp.float32)
        grad_group = dscore[:, :GROUP]
        grad_hard = dscore[:, GROUP:]
        query_grad = score_scale * (jnp.einsum('ic,icd->id', grad_group, group_rows, precision=lax.Precision.HIGHEST) + jnp.einsum('ik,ikd->id', grad_hard, hard_rows, precision=lax.Precision.HIGHEST))
        dense_grad = jnp.zeros((QD, N_PA * IB), jnp.float32).at[query_index[:, None], chosen].add(grad_group)
        batch_part = score_scale * jnp.dot(dense_grad.T, query_wide, precision=lax.Precision.HIGHEST)
        batch_part = batch_part.reshape(N_PA, 1, IB, D)
        zero_index = jnp.zeros((), jnp.int32)
        start = (zero_index, col_index, zero_index, zero_index)
        current = lax.dynamic_slice(batch_grad, start, (N_PA, 1, IB, D))
        batch_grad = lax.dynamic_update_slice(batch_grad, current + batch_part, start)
        contrib = score_scale * grad_hard[:, :, None] * query_wide[:, None, :]
        contrib = lax.optimization_barrier(contrib.astype(jnp.bfloat16)).astype(jnp.float32)
        global_rows = (row_index * (N_PB * PD) + hard_block).astype(jnp.int32)
        pool_grad = pool_grad.at[global_rows.reshape(-1)].add(contrib.reshape(QD * HN, D))
        return ((batch_grad, pool_grad), query_grad.astype(jnp.bfloat16))
    start_carry = (jnp.zeros((N_PA, N_PB, IB, D), jnp.float32), jnp.zeros((NPOOL, D), jnp.float32))
    device_list = jnp.arange(DEVICES, dtype=jnp.int32)
    (batch_grad, pool_grad), grads = lax.scan(one_block, start_carry, (device_list, query_blocks, hard_blocks, group_blocks, label_blocks))
    dims = (((1,), (1,)), ((), ()))
    batch_low = batch_grad.reshape(NB, D).astype(jnp.bfloat16)
    pool_low = pool_grad.astype(jnp.bfloat16)
    batch_hidden_grad = lax.dot_general(batch_low, projection, dims, preferred_element_type=jnp.float32).astype(jnp.bfloat16)
    pool_hidden_grad = lax.dot_general(pool_low, projection, dims, preferred_element_type=jnp.float32).astype(jnp.bfloat16)
    return (grads.reshape(NQ, D), batch_hidden_grad, pool_hidden_grad)
```

```python
import math

import jax
import jax.numpy as jnp
from jax import lax
from jax.experimental import pallas as pl
from jax.experimental.pallas import tpu as pltpu
from jax.sharding import PartitionSpec as P

MESH = pl.DeviceIdType.MESH
NX, NY, NZ = 4, 8, 8
D = 1024
QD = 128
PD = 512
IB = 16
NG = 64
GS = 64
HN = 16
NB = NX * NY * IB
SLAB = NY * IB
SUB = QD // 2
SCALE = 1.0 / math.sqrt(D)
F32 = jnp.float32
BF16 = jnp.bfloat16
LOW = -3.0e38

MIRROR = (0, 2, 1, 4, 3, 6, 5, 7)


def slot_of(direction, hops):
    if hops == 0:
        return 0
    if hops == 4:
        return 7
    return 2 * hops - 1 if direction == 0 else 2 * hops


def slot_shift(slot):
    if slot == 7:
        return 4
    hops = (slot + 1) // 2
    return (-hops if slot % 2 else hops) % NZ


def dot(a, b):
    return jnp.dot(a, b, preferred_element_type=F32)


def dot_nt(a, b):
    return lax.dot_general(a, b, (((1,), (1,)), ((), ())), preferred_element_type=F32)


def eye(n):
    same = lax.broadcasted_iota(jnp.int32, (n, n), 0) == lax.broadcasted_iota(jnp.int32, (n, n), 1)
    return jnp.where(same, 1.0, 0.0).astype(BF16)


def turn_ids(ids):
    high = (ids // 128).astype(F32).astype(BF16)
    low = (ids % 128).astype(F32).astype(BF16)
    one = eye(ids.shape[1])
    return (dot_nt(one, high) * 128.0 + dot_nt(one, low)).astype(jnp.int32)


def kernel(
    q_hbm, bh_hbm, ph_hbm, proj_hbm, ids_ref, group_ref, label_ref, lists_ref,
    qg_out, bg_out, pg_out,
    qbuf, proj, bh, ph, pool, column, ot, mask, dense, chosen,
    ids_byz, ids_in, hs_out, hs_in, d_out, d_in, rows16, idcol, dcol,
    t_buf, o_buf, rs_out, rs_in, dg, part, xr_out, xr_in, xsum, y_out, y_in, gterm,
    contrib, g_send, g_recv, g_own, gb, qg_stage, bg_stage, pg_stage,
    ld_sem, st_sem, ag_s, ag_r, rs_s, rs_r, xa_s, xa_r, xr_s, xr_r, one_s, one_r,
):
    pa = lax.axis_index("pa")
    pb = lax.axis_index("pb")
    x, y = pa // NY, pa % NY
    z, core = pb // 2, pb % 2

    def at_z(shift):
        return (pa, ((z + shift + NZ) % NZ) * 2 + core)

    def at_y(shift):
        return (x * NY + (y + shift) % NY, pb)

    def at_x(shift):
        return (((x + shift + NX) % NX) * NY + y, pb)

    partner = (pa, z * 2 + 1 - core)

    def remote(src, dst, send, recv, device):
        return pltpu.make_async_remote_copy(
            src_ref=src, dst_ref=dst, send_sem=send, recv_sem=recv, device_id=device, device_id_type=MESH
        )

    barrier = pltpu.get_barrier_semaphore()
    peers = [at_z(s) for s in range(1, NZ)] + [at_y(s) for s in range(1, NY)] + [at_x(1), at_x(-1), partner]
    for peer in peers:
        pl.semaphore_signal(barrier, inc=1, device_id=peer, device_id_type=MESH)

    loads = [
        pltpu.make_async_copy(q_hbm, qbuf.at[0], ld_sem.at[0]),
        pltpu.make_async_copy(bh_hbm, bh, ld_sem.at[1]),
        pltpu.make_async_copy(proj_hbm, proj, ld_sem.at[2]),
        pltpu.make_async_copy(ph_hbm, ph, ld_sem.at[3]),
    ]
    for load in loads:
        load.start()

    turned = turn_ids(ids_ref[...]) - lax.broadcasted_iota(jnp.int32, (HN, QD), 0) * PD
    for owner_z in range(NZ):
        ids_byz[owner_z] = turned[2 * owner_z : 2 * owner_z + 2, :]
    ids_in[0] = ids_byz[z]

    loads[0].wait()
    pl.semaphore_wait(barrier, len(peers))

    def ag(direction, n):
        hops = n // 2
        rows = pl.ds((direction if n % 2 == 0 else 1 - direction) * SUB, SUB)
        return remote(
            qbuf.at[slot_of(direction, hops), rows],
            qbuf.at[slot_of(direction, hops + 1), rows],
            ag_s.at[direction, n],
            ag_r.at[direction, n],
            at_z(1 if direction == 0 else -1),
        )

    def ag_send(n):
        for direction in (0, 1):
            ag(direction, n).start()

    def ag_arrive(n):
        for direction in (0, 1):
            ag(direction, n).wait_recv()
            if n + 2 <= 6:
                ag(direction, n + 2).start()

    ag_send(0)
    ag_send(1)

    def small(src, dst, which, slot):
        return remote(src, dst.at[MIRROR[slot]], one_s.at[which], one_r.at[which], at_z(slot_shift(slot)))

    def small_wait(buf, sem):
        pltpu.make_async_copy(buf.at[pl.ds(1, NZ - 1)], buf.at[pl.ds(1, NZ - 1)], sem).wait()

    for slot in range(1, NZ):
        small(ids_byz.at[(z + slot_shift(slot)) % NZ], ids_in, 0, slot).start()

    loads[1].wait()
    loads[2].wait()
    own_rows = pl.ds(pl.multiple_of(pa * IB, IB), IB)

    def batch_tile(i, carry):
        cols = pl.ds(pl.multiple_of(i * 256, 256), 256)
        column[own_rows, cols] = dot(bh[...], proj[:, cols]).astype(BF16)
        return carry

    lax.fori_loop(0, 4, batch_tile, 0)
    for shift in range(1, NY):
        remote(column.at[own_rows], column.at[own_rows], one_s.at[3], one_r.at[3], at_y(shift)).start()

    loads[3].wait()
    pool_rows = pl.ds(pl.multiple_of(core * PD, PD), PD)

    def pool_tile(i, carry):
        cols = pl.ds(pl.multiple_of(i * 256, 256), 256)
        pool[pool_rows, cols] = dot(ph[...], proj[:, cols]).astype(BF16)
        return carry

    lax.fori_loop(0, 4, pool_tile, 0)
    pool_swap = remote(pool.at[pool_rows], pool.at[pool_rows], one_s.at[5], one_r.at[5], partner)
    pool_swap.start()

    ag_arrive(0)

    lists_turned = lists_ref[...]
    high = (lists_turned // 32).astype(F32).astype(BF16)
    low = (lists_turned % 32).astype(F32).astype(BF16)
    one = eye(NG)
    high = dot_nt(one, high).astype(BF16)
    low = dot_nt(one, low).astype(BF16)
    in_group = lax.broadcasted_iota(jnp.int32, (NG, QD), 0) == group_ref[...]
    in_group = jnp.where(in_group, 1.0, 0.0).astype(BF16)
    chosen[...] = (dot(high, in_group) * 32.0 + dot(low, in_group)).astype(jnp.int32)
    at_label = lax.broadcasted_iota(jnp.int32, (GS, QD), 0) == label_ref[...]
    label_row = jnp.sum(jnp.where(at_label, chosen[...], 0), axis=0, keepdims=True)

    def mask_tile(i, carry):
        base = pl.multiple_of(i * 64, 64)
        row = lax.broadcasted_iota(jnp.int32, (64, QD), 0) + base
        found = jnp.zeros((64, QD), F32)
        for c in range(GS):
            found = jnp.where(row == chosen[c : c + 1, :], 1.0, found)
        mask[pl.ds(base, 64), :] = found
        return carry

    lax.fori_loop(0, NB // 64, mask_tile, 0)

    def slab(shift, half):
        start = ((x + shift + NX) % NX) * SLAB + half * (SLAB // 2)
        return pl.ds(pl.multiple_of(start, SLAB // 2), SLAB // 2)

    def xa(direction, n):
        half = direction if n % 2 == 0 else 1 - direction
        sign = 1 if direction == 0 else -1
        rows = slab(0 if n < 2 else -sign, half)
        return remote(column.at[rows], column.at[rows], xa_s.at[direction, n], xa_r.at[direction, n], at_x(sign))

    def y_wait(buf, sem):
        pltpu.make_async_copy(buf, buf, sem).wait()

    y_wait(column.at[pl.ds(0, (NY - 1) * IB)], one_r.at[3])
    for n in (0, 1):
        for direction in (0, 1):
            xa(direction, n).start()

    def xa_arrive(n):
        for direction in (0, 1):
            xa(direction, n).wait_recv()
            if n == 0:
                xa(direction, 2).start()

    def score(slot, count):
        queries = qbuf[slot : slot + count].reshape(count * QD, D)
        for k in (0, 1):

            def tile(i, carry):
                base = pl.multiple_of(i * 256, 256)
                rows = pl.ds(pl.multiple_of(k * PD + base, 256), 256)
                scores = dot_nt(pool[rows, :], queries)
                iota = lax.broadcasted_iota(jnp.int32, (256, QD), 0) + base
                new = []
                for j in range(count):
                    hit = iota == ids_in[slot + j, k : k + 1, :]
                    ot[rows, (slot + j) * QD : (slot + j + 1) * QD] = jnp.where(hit, 1.0, 0.0).astype(BF16)
                    found = jnp.where(hit, scores[:, j * QD : (j + 1) * QD], 0.0)
                    new.append(carry[j] + jnp.sum(found, axis=0, keepdims=True))
                return tuple(new)

            sums = lax.fori_loop(0, 2, tile, tuple(jnp.zeros((1, QD), F32) for _ in range(count)))
            for j in range(count):
                target = hs_in if slot == 0 else hs_out
                target[slot + j, k : k + 1, :] = sums[j] * SCALE
        for j in range(count):
            if slot > 0:
                small(hs_out.at[slot + j], hs_in, 1, slot + j).start()

    ag_arrive(1)
    small_wait(ids_in, one_r.at[0])
    pool_swap.wait_recv()
    score(0, 1)
    ag_arrive(2)
    score(1, 2)
    xa_arrive(0)
    ag_arrive(3)
    score(3, 2)
    for slot in range(NZ):
        rows16[2 * slot : 2 * slot + 2, :] = ids_in[slot].astype(F32)
    idcol[...] = turn_rows(rows16[...])
    ag_arrive(4)
    ag_arrive(5)
    score(5, 2)
    xa_arrive(1)
    xa_arrive(2)

    def dense_tile(i, carry):
        rows = pl.ds(pl.multiple_of(i * 256, 256), 256)
        value = dot_nt(column[rows, :], qbuf[0]) * SCALE
        dense[rows, :] = jnp.where(mask[rows, :] > 0.0, value, LOW)
        return carry

    lax.fori_loop(0, NB // 256, dense_tile, 0)
    group_max = jnp.max(dense[...], axis=0, keepdims=True)
    ag_arrive(6)
    score(7, 1)

    small_wait(hs_in, one_r.at[1])
    hard = hs_in[...]
    top = jnp.maximum(group_max, jnp.max(jnp.max(hard, axis=0), axis=0, keepdims=True))
    hard = jnp.exp(hard - top[None])
    likely = jnp.where(mask[...] > 0.0, jnp.exp(dense[...] - top), 0.0)
    total = jnp.sum(likely, axis=0, keepdims=True) + jnp.sum(jnp.sum(hard, axis=0), axis=0, keepdims=True)
    d_hard = (hard / total[None]).astype(BF16).astype(F32)
    d_out[...] = d_hard
    d_in[0] = d_hard[0]
    for slot in range(1, NZ):
        small(d_out.at[slot], d_in, 2, slot).start()
    target = jnp.where(lax.broadcasted_iota(jnp.int32, (NB, QD), 0) == label_row, 1.0, 0.0)
    dg[...] = (likely / total - target).astype(BF16)

    def part_tile(i, carry):
        cols = pl.ds(pl.multiple_of(i * 256, 256), 256)
        part[:, cols] = dot(dg[...], qbuf[0, :, cols]) * SCALE
        return carry

    lax.fori_loop(0, 4, part_tile, 0)

    def xr(direction, n):
        return remote(
            xr_out.at[direction, n],
            xr_in.at[direction, n],
            xr_s.at[direction, n],
            xr_r.at[direction, n],
            at_x(1 if direction == 0 else -1),
        )

    def xr_send(n):
        for direction in (0, 1):
            half = direction if n % 2 == 0 else 1 - direction
            sign = 1 if direction == 0 else -1
            value = part[slab(2 if n == 0 else sign, half), :]
            if n == 2:
                xr(direction, 0).wait_recv()
                value = value + xr_in[direction, 0].astype(F32)
            xr_out[direction, n] = value.astype(BF16)
            xr(direction, n).start()

    xr_send(0)
    xr_send(1)

    def rs(direction, n):
        return remote(
            rs_out.at[direction, n],
            rs_in.at[direction, n],
            rs_s.at[direction, n],
            rs_r.at[direction, n],
            at_z(1 if direction == 0 else -1),
        )

    def rs_send(n):
        hops = 4 - (n + 1) // 2
        for direction in (0, 1):
            half = direction if n % 2 == 0 else 1 - direction
            value = t_buf[slot_of(1 - direction, hops), half * SUB : (half + 1) * SUB, :]
            if n >= 2:
                rs(direction, n - 2).wait_recv()
                value = value + rs_in[direction, n - 2].astype(F32)
            rs_out[direction, n] = value.astype(BF16)
            rs(direction, n).start()

    def terms(slot, count):
        lane = lax.broadcasted_iota(jnp.int32, (QD, PD), 1)
        for j in range(count):
            for k in (0, 1):
                at = 2 * (slot + j) + k
                hit = lane == idcol[:, at : at + 1]
                value = jnp.where(hit, dcol[:, at : at + 1], 0.0)
                o_buf[j * QD : (j + 1) * QD, k * PD : (k + 1) * PD] = value.astype(BF16)

        def tile(i, carry):
            cols = pl.ds(pl.multiple_of(i * 256, 256), 256)
            value = dot(o_buf[0 : count * QD, :], pool[:, cols])
            for j in range(count):
                t_buf[slot + j, :, cols] = value[j * QD : (j + 1) * QD]
            return carry

        lax.fori_loop(0, 4, tile, 0)

    small_wait(d_in, one_r.at[2])
    for slot in range(NZ):
        rows16[2 * slot : 2 * slot + 2, :] = d_in[slot]
    dcol[...] = dot_nt(eye(QD), rows16[...].astype(BF16))
    terms(7, 1)
    rs_send(0)
    terms(5, 2)
    rs_send(1)

    dg_turned = dot_nt(eye(QD), dg[...]).astype(BF16)

    def group_tile(i, carry):
        cols = pl.ds(pl.multiple_of(i * 256, 256), 256)
        gterm[:, cols] = dot(dg_turned, column[:, cols])
        return carry

    lax.fori_loop(0, 4, group_tile, 0)
    xr_send(2)
    terms(3, 2)
    rs_send(2)
    terms(1, 2)
    terms(0, 1)
    rs_send(3)

    def contribs(k):
        for slot in range(NZ):
            at = 2 * slot
            weight = jnp.where(k == 0, dcol[:, at : at + 1], dcol[:, at + 1 : at + 2]) * SCALE
            contrib[slot * QD : (slot + 1) * QD, :] = (qbuf[slot].astype(F32) * weight).astype(BF16)

    def pool_sum(k, target, first, last):
        def tile(i, carry):
            cols = pl.ds(pl.multiple_of(i * 256, 256), 256)
            target[:, cols] = dot(ot[pl.ds(pl.multiple_of(k * PD, PD), PD), :], contrib[:, cols])
            return carry

        lax.fori_loop(first, last, tile, 0)

    contribs(1 - core)
    rs_send(4)
    pool_sum(1 - core, g_send, 0, 4)
    g_swap = remote(g_send, g_recv, one_s.at[6], one_r.at[6], partner)
    g_swap.start()
    rs_send(5)

    for direction in (0, 1):
        xr(direction, 1).wait_recv()
        xr(direction, 2).wait_recv()
    for half in (0, 1):
        value = part[slab(0, half), :]
        value = value + xr_in[half, 2].astype(F32) + xr_in[1 - half, 1].astype(F32)
        xsum[half * 4 : half * 4 + 4] = value.reshape(NY // 2, IB, D)
        y_out[half * 4 : half * 4 + 4] = value.astype(BF16).reshape(NY // 2, IB, D)
    for shift in range(1, NY):
        remote(
            y_out.at[(y + shift) % NY], y_in.at[shift], one_s.at[4], one_r.at[4], at_y(shift)
        ).start()
    contribs(core)
    rs_send(6)
    pool_sum(core, g_own, 0, 4)
    g_swap.wait_recv()
    gb[...] = (g_own[...] + g_recv[...]).astype(BF16)

    def pool_out(i, carry):
        cols = pl.ds(pl.multiple_of(i * 256, 256), 256)
        pg_stage[:, cols] = dot_nt(gb[...], proj[cols, :]).astype(BF16)
        return carry

    lax.fori_loop(0, 4, pool_out, 0)
    pg_store = pltpu.make_async_copy(pg_stage, pg_out, st_sem.at[0])
    pg_store.start()

    y_wait(y_in.at[pl.ds(1, NY - 1)], one_r.at[4])
    value = xsum[y]
    for shift in range(1, NY):
        value = value + y_in[shift].astype(F32)
    value = value.astype(BF16)

    def batch_out(i, carry):
        cols = pl.ds(pl.multiple_of(i * 256, 256), 256)
        bg_stage[:, cols] = dot_nt(value, proj[cols, :]).astype(BF16)
        return carry

    lax.fori_loop(0, 4, batch_out, 0)
    bg_store = pltpu.make_async_copy(bg_stage, bg_out, st_sem.at[1])
    bg_store.start()

    for direction in (0, 1):
        rs(direction, 5).wait_recv()
        rs(direction, 6).wait_recv()
    for half in (0, 1):
        rows = slice(half * SUB, (half + 1) * SUB)
        value = gterm[rows, :] + t_buf[0, rows, :]
        value = value + (rs_in[half, 6].astype(F32) + rs_in[1 - half, 5].astype(F32))
        qg_stage[rows, :] = (value * SCALE).astype(BF16)
    qg_store = pltpu.make_async_copy(qg_stage, qg_out, st_sem.at[2])
    qg_store.start()

    for direction in (0, 1):
        for n in range(7):
            ag(direction, n).wait_send()
            rs(direction, n).wait_send()
        for n in range(3):
            xa(direction, n).wait_send()
            xr(direction, n).wait_send()
    small_wait(ids_in, one_s.at[0])
    small_wait(hs_in, one_s.at[1])
    small_wait(d_in, one_s.at[2])
    y_wait(column.at[pl.ds(0, (NY - 1) * IB)], one_s.at[3])
    y_wait(y_in.at[pl.ds(1, NY - 1)], one_s.at[4])
    pool_swap.wait_send()
    g_swap.wait_send()
    pg_store.wait()
    bg_store.wait()
    qg_store.wait()


def turn_rows(rows):
    high = jnp.floor(rows * (1.0 / 32.0))
    low = rows - high * 32.0
    one = eye(QD)
    turned = dot_nt(one, high.astype(BF16)) * 32.0 + dot_nt(one, low.astype(BF16))
    return turned.astype(jnp.int32)


def shards(queries, batch_hidden, pool_hidden, projection, hard_ids, query_group, labels, group_lists):
    hbm = pl.BlockSpec(memory_space=pl.ANY)
    vmem = pl.BlockSpec(memory_space=pltpu.VMEM)
    dma = pltpu.SemaphoreType.DMA
    scratch = [
        pltpu.VMEM((NZ, QD, D), BF16),
        pltpu.VMEM((D, D), BF16),
        pltpu.VMEM((IB, D), BF16),
        pltpu.VMEM((PD, D), BF16),
        pltpu.VMEM((2 * PD, D), BF16),
        pltpu.VMEM((NB, D), BF16),
        pltpu.VMEM((2 * PD, NZ * QD), BF16),
        pltpu.VMEM((NB, QD), F32),
        pltpu.VMEM((NB, QD), F32),
        pltpu.VMEM((GS, QD), jnp.int32),
        pltpu.VMEM((NZ, 2, QD), jnp.int32),
        pltpu.VMEM((NZ, 2, QD), jnp.int32),
        pltpu.VMEM((NZ, 2, QD), F32),
        pltpu.VMEM((NZ, 2, QD), F32),
        pltpu.VMEM((NZ, 2, QD), F32),
        pltpu.VMEM((NZ, 2, QD), F32),
        pltpu.VMEM((HN, QD), F32),
        pltpu.VMEM((QD, HN), jnp.int32),
        pltpu.VMEM((QD, HN), F32),
        pltpu.VMEM((NZ, QD, D), F32),
        pltpu.VMEM((2 * QD, 2 * PD), BF16),
        pltpu.VMEM((2, 7, SUB, D), BF16),
        pltpu.VMEM((2, 7, SUB, D), BF16),
        pltpu.VMEM((NB, QD), BF16),
        pltpu.VMEM((NB, D), F32),
        pltpu.VMEM((2, 3, SLAB // 2, D), BF16),
        pltpu.VMEM((2, 3, SLAB // 2, D), BF16),
        pltpu.VMEM((NY, IB, D), F32),
        pltpu.VMEM((NY, IB, D), BF16),
        pltpu.VMEM((NY, IB, D), BF16),
        pltpu.VMEM((QD, D), F32),
        pltpu.VMEM((NZ * QD, D), BF16),
        pltpu.VMEM((PD, D), F32),
        pltpu.VMEM((PD, D), F32),
        pltpu.VMEM((PD, D), F32),
        pltpu.VMEM((PD, D), BF16),
        pltpu.VMEM((QD, D), BF16),
        pltpu.VMEM((IB, D), BF16),
        pltpu.VMEM((PD, D), BF16),
        dma((4,)),
        dma((3,)),
        dma((2, 7)),
        dma((2, 7)),
        dma((2, 7)),
        dma((2, 7)),
        dma((2, 3)),
        dma((2, 3)),
        dma((2, 3)),
        dma((2, 3)),
        dma((7,)),
        dma((7,)),
    ]
    return pl.pallas_call(
        kernel,
        out_shape=(
            jax.ShapeDtypeStruct((QD, D), BF16),
            jax.ShapeDtypeStruct((IB, D), BF16),
            jax.ShapeDtypeStruct((PD, D), BF16),
        ),
        in_specs=[hbm] * 4 + [vmem] * 4,
        out_specs=(hbm, hbm, hbm),
        scratch_shapes=scratch,
        compiler_params=pltpu.CompilerParams(
            collective_id=0, has_side_effects=True, vmem_limit_bytes=56 * 1024 * 1024
        ),
        cost_estimate=pl.CostEstimate(flops=9_000_000_000, bytes_accessed=6_000_000, transcendentals=100_000),
    )(
        queries, batch_hidden, pool_hidden, projection, hard_ids,
        query_group.reshape(1, QD), labels.reshape(1, QD), group_lists,
    )


def solution(mesh):
    return jax.shard_map(
        shards,
        mesh=mesh,
        in_specs=(
            P(("pa", "pb"), None),
            P(("pa", "pb"), None),
            P(("pa", "pb"), None),
            P(),
            P(("pa", "pb"), None),
            P(("pa", "pb")),
            P(("pa", "pb")),
            P(),
        ),
        out_specs=(P(("pa", "pb"), None), P(("pa", "pb"), None), P(("pa", "pb"), None)),
        check_vma=False,
    )
```

```python
import math

import jax
import jax.numpy as jnp
from jax import lax
from jax.experimental import pallas as pl
from jax.experimental.pallas import tpu as pltpu
from jax.sharding import PartitionSpec as P

MESH = pl.DeviceIdType.MESH
NX, NY, NZ = 4, 8, 8
D = 1024
QD = 128
PD = 512
IB = 16
NG = 64
GS = 64
HN = 16
NB = NX * NY * IB
SLAB = NY * IB
SUB = QD // 2
HD = D // 2
SCALE = 1.0 / math.sqrt(D)
F32 = jnp.float32
BF16 = jnp.bfloat16
LOW = -3.0e38

MIRROR = (0, 1, 3, 2, 5, 4, 7, 6)


def slot_of(direction, hops):
    if hops == 0:
        return 0
    if hops == 4:
        return 1
    return 2 * hops + direction


def slot_shift(slot):
    if slot < 2:
        return 4 * slot
    hops = slot // 2
    return (hops if slot % 2 else -hops) % NZ


def dot(a, b):
    return jnp.dot(a, b, preferred_element_type=F32)


def dot_nt(a, b):
    return lax.dot_general(a, b, (((1,), (1,)), ((), ())), preferred_element_type=F32)


def eye(n):
    same = lax.broadcasted_iota(jnp.int32, (n, n), 0) == lax.broadcasted_iota(jnp.int32, (n, n), 1)
    return jnp.where(same, 1.0, 0.0).astype(BF16)


def turn_rows(rows):
    high = jnp.floor(rows * (1.0 / 32.0))
    low = rows - high * 32.0
    one = eye(QD)
    turned = dot_nt(one, high.astype(BF16)) * 32.0 + dot_nt(one, low.astype(BF16))
    return turned.astype(jnp.int32)


def kernel(
    q_hbm, bh_hbm, ph_hbm, proj_hbm, ids_ref, group_ref, label_ref, lists_ref,
    qg_out, bg_out, pg_out,
    qbuf, proj, bh, ph, pool, column, ot, mask, dense, chosen,
    ids_byz, ids_in, hs_out, hs_in, d_out, d_in, rows16, idcol, dcol,
    t_buf, o_buf, rs_out, rs_in, dg, part, xr_out, xr_in, xsum, y_out, y_in, gterm,
    contrib, g_send, g_recv, g_own, gb,
    ld_sem, ag_s, ag_r, rs_s, rs_r, xa_s, xa_r, xr_s, xr_r, one_s, one_r, z_ready, xy_ready,
):
    pa = lax.axis_index("pa")
    pb = lax.axis_index("pb")
    x, y = pa // NY, pa % NY
    z, core = pb // 2, pb % 2

    def at_z(shift):
        return (pa, ((z + shift + NZ) % NZ) * 2 + core)

    def at_y(shift):
        return (x * NY + (y + shift) % NY, pb)

    def at_x(shift):
        return (((x + shift + NX) % NX) * NY + y, pb)

    partner = (pa, z * 2 + 1 - core)

    def remote(src, dst, send, recv, device):
        return pltpu.make_async_remote_copy(
            src_ref=src, dst_ref=dst, send_sem=send, recv_sem=recv, device_id=device, device_id_type=MESH
        )

    barrier = pltpu.get_barrier_semaphore()

    def hello(device):
        pl.semaphore_signal(barrier, inc=1, device_id=device, device_id_type=MESH)

    for shift in range(1, NZ):
        hello((pa, ((z + shift) % NZ) * 2))
    hello(partner)
    for shift in range(1, NY):
        hello((x * NY + (y + shift) % NY, z * 2 + 1))
    for shift in (1, NX - 1):
        hello((((x + shift) % NX) * NY + y, z * 2 + 1))

    loads = [
        pltpu.make_async_copy(q_hbm, qbuf.at[0], ld_sem.at[0]),
        pltpu.make_async_copy(bh_hbm, bh, ld_sem.at[1]),
        pltpu.make_async_copy(proj_hbm, proj, ld_sem.at[2]),
        pltpu.make_async_copy(ph_hbm, ph, ld_sem.at[3]),
    ]
    for load in loads:
        load.start()
    loads[0].wait()

    @pl.when(core == 0)
    def _():
        pl.semaphore_wait(barrier, 2 * (NZ - 1) + 1)
        pl.semaphore_signal(z_ready, inc=1, device_id=partner, device_id_type=MESH)

    @pl.when(core == 1)
    def _():
        pl.semaphore_wait(z_ready, 1)

    def ag(direction, n):
        hops = n // 2
        rows = pl.ds((direction if n % 2 == 0 else 1 - direction) * SUB, SUB)
        return remote(
            qbuf.at[slot_of(direction, hops), rows],
            qbuf.at[slot_of(direction, hops + 1), rows],
            ag_s.at[direction, n],
            ag_r.at[direction, n],
            at_z(1 if direction == 0 else -1),
        )

    def ag_arrive(n):
        for direction in (0, 1):
            ag(direction, n).wait_recv()
            if n + 2 <= 6:
                ag(direction, n + 2).start()

    for n in (0, 1):
        for direction in (0, 1):
            ag(direction, n).start()

    def small(src, dst, which, slot):
        return remote(src, dst.at[MIRROR[slot]], one_s.at[which], one_r.at[which], at_z(slot_shift(slot)))

    def small_wait(buf, sem):
        pltpu.make_async_copy(buf.at[pl.ds(1, NZ - 1)], buf.at[pl.ds(1, NZ - 1)], sem).wait()

    loads[1].wait()
    loads[2].wait()
    own_rows = pl.ds(pl.multiple_of(pa * IB, IB), IB)

    def batch_half(half):
        def tile(i, carry):
            cols = pl.ds(pl.multiple_of(i * 256, 256), 256)
            wide = pl.ds(pl.multiple_of(half * HD + i * 256, 256), 256)
            column[half, own_rows, cols] = dot(bh[...], proj[:, wide]).astype(BF16)
            return carry

        lax.fori_loop(0, 2, tile, 0)

    def ya_send(half):
        here = column.at[half, own_rows]
        for shift in range(1, NY):
            remote(here, here, one_s.at[9 + half], one_r.at[9 + half], at_y(shift)).start()

    batch_half(0)

    @pl.when(core == 1)
    def _():
        pl.semaphore_wait(barrier, 2 * (NY - 1) + 2 * 2 + 1)
        pl.semaphore_signal(xy_ready, inc=1, device_id=partner, device_id_type=MESH)

    @pl.when(core == 0)
    def _():
        pl.semaphore_wait(xy_ready, 1)

    ya_send(0)
    batch_half(1)
    ya_send(1)

    local_rows = ids_ref[...] - lax.broadcasted_iota(jnp.int32, (HN, QD), 0) * PD
    for owner_z in range(NZ):
        ids_byz[owner_z] = local_rows[2 * owner_z : 2 * owner_z + 2, :]
    ids_in[0] = ids_byz[z]
    for slot in range(1, NZ):
        small(ids_byz.at[(z + slot_shift(slot)) % NZ], ids_in, 0, slot).start()

    ag_arrive(0)
    loads[3].wait()
    pool_rows = pl.ds(pl.multiple_of(core * PD, PD), PD)

    def pool_tile(i, carry):
        cols = pl.ds(pl.multiple_of(i * 256, 256), 256)
        pool[pool_rows, cols] = dot(ph[...], proj[:, cols]).astype(BF16)
        return carry

    lax.fori_loop(0, 4, pool_tile, 0)
    pool_swap = remote(pool.at[pool_rows], pool.at[pool_rows], one_s.at[7], one_r.at[7], partner)
    pool_swap.start()
    ag_arrive(1)

    lists_turned = lists_ref[...]
    high = (lists_turned // 32).astype(F32).astype(BF16)
    low = (lists_turned % 32).astype(F32).astype(BF16)
    one = eye(NG)
    high = dot_nt(one, high).astype(BF16)
    low = dot_nt(one, low).astype(BF16)
    in_group = lax.broadcasted_iota(jnp.int32, (NG, QD), 0) == group_ref[...]
    in_group = jnp.where(in_group, 1.0, 0.0).astype(BF16)
    chosen[...] = (dot(high, in_group) * 32.0 + dot(low, in_group)).astype(jnp.int32)
    at_label = lax.broadcasted_iota(jnp.int32, (GS, QD), 0) == label_ref[...]
    label_row = jnp.sum(jnp.where(at_label, chosen[...], 0), axis=0, keepdims=True)

    def mask_tile(i, carry):
        base = pl.multiple_of(i * 64, 64)
        row = lax.broadcasted_iota(jnp.int32, (64, QD), 0) + base
        found = jnp.zeros((64, QD), F32)
        for c in range(GS):
            found = jnp.where(row == chosen[c : c + 1, :], 1.0, found)
        mask[pl.ds(base, 64), :] = found
        return carry

    def slab(shift, half):
        start = ((x + shift + NX) % NX) * SLAB + half * (SLAB // 2)
        return pl.ds(pl.multiple_of(start, SLAB // 2), SLAB // 2)

    def xa(part_of, direction, n):
        half = direction if n % 2 == 0 else 1 - direction
        sign = 1 if direction == 0 else -1
        here = column.at[part_of, slab(0 if n < 2 else -sign, half)]
        return remote(here, here, xa_s.at[part_of, direction, n], xa_r.at[part_of, direction, n], at_x(sign))

    def all_wait(buf, sem):
        pltpu.make_async_copy(buf, buf, sem).wait()

    def xa_send(part_of):
        all_wait(column.at[part_of, pl.ds(0, (NY - 1) * IB)], one_r.at[9 + part_of])
        for n in (0, 1):
            for direction in (0, 1):
                xa(part_of, direction, n).start()

    def xa_arrive(part_of, n):
        for direction in (0, 1):
            xa(part_of, direction, n).wait_recv()
            if n == 0:
                xa(part_of, direction, 2).start()

    xa_send(0)
    lax.fori_loop(0, NB // 128, mask_tile, 0)
    ag_arrive(2)
    xa_send(1)
    small_wait(ids_in, one_r.at[0])
    for slot in range(NZ):
        rows16[2 * slot : 2 * slot + 2, :] = ids_in[slot].astype(F32)
    idcol[...] = turn_rows(rows16[...])
    pool_swap.wait_recv()

    def score(slot):
        queries = qbuf[slot : slot + 2].reshape(2 * QD, D)
        for k in (0, 1):

            def tile(i, carry):
                base = pl.multiple_of(i * 256, 256)
                rows = pl.ds(pl.multiple_of(k * PD + base, 256), 256)
                scores = dot_nt(pool[rows, :], queries)
                iota = lax.broadcasted_iota(jnp.int32, (256, QD), 0) + base
                new = []
                for j in (0, 1):
                    hit = iota == ids_in[slot + j, k : k + 1, :]
                    ot[rows, (slot + j) * QD : (slot + j + 1) * QD] = jnp.where(hit, 1.0, 0.0).astype(BF16)
                    found = jnp.where(hit, scores[:, j * QD : (j + 1) * QD], 0.0)
                    new.append(carry[j] + jnp.sum(found, axis=0, keepdims=True))
                return tuple(new)

            sums = lax.fori_loop(0, 2, tile, tuple(jnp.zeros((1, QD), F32) for _ in (0, 1)))
            for j in (0, 1):
                target = hs_in if slot + j == 0 else hs_out
                target[slot + j, k : k + 1, :] = sums[j] * SCALE
        for j in (0, 1):
            if slot + j > 0:
                small(hs_out.at[slot + j], hs_in, 1, slot + j).start()

    def dense_half(half):
        def tile(i, carry):
            rows = pl.ds(pl.multiple_of(i * 256, 256), 256)
            value = dot_nt(column[half, rows, :], qbuf[0, :, half * HD : (half + 1) * HD])
            if half == 0:
                dense[rows, :] = value
            else:
                value = (dense[rows, :] + value) * SCALE
                dense[rows, :] = jnp.where(mask[rows, :] > 0.0, value, LOW)
            return carry

        lax.fori_loop(0, NB // 256, tile, 0)

    score(2)
    ag_arrive(3)
    xa_arrive(0, 0)
    score(4)
    ag_arrive(4)
    lax.fori_loop(NB // 128, NB // 64, mask_tile, 0)
    xa_arrive(1, 0)
    ag_arrive(5)
    score(6)
    xa_arrive(0, 1)
    xa_arrive(0, 2)
    dense_half(0)
    ag_arrive(6)
    score(0)
    xa_arrive(1, 1)
    xa_arrive(1, 2)
    dense_half(1)

    group_max = jnp.max(dense[...], axis=0, keepdims=True)
    small_wait(hs_in, one_r.at[1])
    hard = hs_in[...]
    top = jnp.maximum(group_max, jnp.max(jnp.max(hard, axis=0), axis=0, keepdims=True))
    hard = jnp.exp(hard - top[None])
    likely = jnp.where(mask[...] > 0.0, jnp.exp(dense[...] - top), 0.0)
    total = jnp.sum(likely, axis=0, keepdims=True) + jnp.sum(jnp.sum(hard, axis=0), axis=0, keepdims=True)
    d_hard = (hard / total[None]).astype(BF16).astype(F32)
    d_out[...] = d_hard
    d_in[0] = d_hard[0]
    for slot in range(1, NZ):
        small(d_out.at[slot], d_in, 3, slot).start()
    target = jnp.where(lax.broadcasted_iota(jnp.int32, (NB, QD), 0) == label_row, 1.0, 0.0)
    dg[...] = (likely / total - target).astype(BF16)

    def rs(direction, n):
        return remote(
            rs_out.at[direction, n],
            rs_in.at[direction, n],
            rs_s.at[direction, n],
            rs_r.at[direction, n],
            at_z(1 if direction == 0 else -1),
        )

    def rs_send(n):
        hops = 4 - (n + 1) // 2
        for direction in (0, 1):
            half = direction if n % 2 == 0 else 1 - direction
            value = t_buf[slot_of(1 - direction, hops), half * SUB : (half + 1) * SUB, :]
            if n >= 2:
                rs(direction, n - 2).wait_recv()
                value = value + rs_in[direction, n - 2].astype(F32)
            rs_out[direction, n] = value.astype(BF16)
            rs(direction, n).start()

    def terms(slot):
        lane = lax.broadcasted_iota(jnp.int32, (QD, PD), 1)
        for j in (0, 1):
            for k in (0, 1):
                at = 2 * (slot + j) + k
                hit = lane == idcol[:, at : at + 1]
                value = jnp.where(hit, dcol[:, at : at + 1], 0.0)
                o_buf[j * QD : (j + 1) * QD, k * PD : (k + 1) * PD] = value.astype(BF16)

        def tile(i, carry):
            cols = pl.ds(pl.multiple_of(i * 256, 256), 256)
            value = dot(o_buf[...], pool[:, cols])
            t_buf[slot, :, cols] = value[0:QD]
            t_buf[slot + 1, :, cols] = value[QD : 2 * QD]
            return carry

        lax.fori_loop(0, 4, tile, 0)

    def part_half(half):
        def tile(i, carry):
            cols = pl.ds(pl.multiple_of(i * 256, 256), 256)
            wide = pl.ds(pl.multiple_of(half * HD + i * 256, 256), 256)
            part[half, :, cols] = dot(dg[...], qbuf[0, :, wide]) * SCALE
            return carry

        lax.fori_loop(0, 2, tile, 0)

    def xr(part_of, direction, n):
        return remote(
            xr_out.at[part_of, direction, n],
            xr_in.at[part_of, direction, n],
            xr_s.at[part_of, direction, n],
            xr_r.at[part_of, direction, n],
            at_x(1 if direction == 0 else -1),
        )

    def xr_send(part_of, n):
        for direction in (0, 1):
            half = direction if n % 2 == 0 else 1 - direction
            sign = 1 if direction == 0 else -1
            value = part[part_of, slab(2 if n == 0 else sign, half), :]
            if n == 2:
                xr(part_of, direction, 0).wait_recv()
                value = value + xr_in[part_of, direction, 0].astype(F32)
            xr_out[part_of, direction, n] = value.astype(BF16)
            xr(part_of, direction, n).start()

    def yr_send(part_of):
        for direction in (0, 1):
            xr(part_of, direction, 1).wait_recv()
            xr(part_of, direction, 2).wait_recv()
        for half in (0, 1):
            value = part[part_of, slab(0, half), :]
            value = value + xr_in[part_of, half, 2].astype(F32) + xr_in[part_of, 1 - half, 1].astype(F32)
            xsum[part_of, half * 4 : half * 4 + 4] = value.reshape(NY // 2, IB, HD)
            y_out[part_of, half * 4 : half * 4 + 4] = value.astype(BF16).reshape(NY // 2, IB, HD)
        for shift in range(1, NY):
            remote(
                y_out.at[part_of, (y + shift) % NY],
                y_in.at[part_of, shift],
                one_s.at[5 + part_of],
                one_r.at[5 + part_of],
                at_y(shift),
            ).start()

    def contribs(which):
        k = 1 - core if which == 0 else core
        for slot in range(NZ):
            at = 2 * slot
            weight = jnp.where(k == 0, dcol[:, at : at + 1], dcol[:, at + 1 : at + 2]) * SCALE
            contrib[which, slot * QD : (slot + 1) * QD, :] = (qbuf[slot].astype(F32) * weight).astype(BF16)

    def pool_sum(which, target, first, last):
        k = 1 - core if which == 0 else core

        def tile(i, carry):
            cols = pl.ds(pl.multiple_of(i * 256, 256), 256)
            target[:, cols] = dot(ot[pl.ds(pl.multiple_of(k * PD, PD), PD), :], contrib[which, :, cols])
            return carry

        lax.fori_loop(first, last, tile, 0)

    def group_term():
        dg_turned = dot_nt(eye(QD), dg[...]).astype(BF16)
        for half in (0, 1):

            def tile(i, carry):
                cols = pl.ds(pl.multiple_of(i * 256, 256), 256)
                wide = pl.ds(pl.multiple_of(half * HD + i * 256, 256), 256)
                gterm[:, wide] = dot(dg_turned, column[half, :, cols])
                return carry

            lax.fori_loop(0, 2, tile, 0)

    part_half(0)
    xr_send(0, 0)
    xr_send(0, 1)
    part_half(1)
    xr_send(1, 0)
    xr_send(1, 1)
    small_wait(d_in, one_r.at[3])
    for slot in range(NZ):
        rows16[2 * slot : 2 * slot + 2, :] = d_in[slot]
    dcol[...] = dot_nt(eye(QD), rows16[...].astype(BF16))
    terms(0)
    rs_send(0)
    terms(6)
    rs_send(1)
    terms(4)
    rs_send(2)
    terms(2)
    xr_send(0, 2)
    rs_send(3)
    xr_send(1, 2)
    contribs(0)
    rs_send(4)
    pool_sum(0, g_send, 0, 4)
    g_swap = remote(g_send, g_recv, one_s.at[8], one_r.at[8], partner)
    g_swap.start()
    yr_send(0)
    rs_send(5)
    yr_send(1)
    rs_send(6)
    contribs(1)
    pool_sum(1, g_own, 0, 4)
    group_term()
    g_swap.wait_recv()
    gb[...] = (g_own[...] + g_recv[...]).astype(BF16)

    def pool_out(i, carry):
        cols = pl.ds(pl.multiple_of(i * 256, 256), 256)
        pg_out[:, cols] = dot_nt(gb[...], proj[cols, :]).astype(BF16)
        return carry

    lax.fori_loop(0, 4, pool_out, 0)

    batch_sum = []
    for half in (0, 1):
        all_wait(y_in.at[half, pl.ds(1, NY - 1)], one_r.at[5 + half])
        value = xsum[half, y]
        for shift in range(1, NY):
            value = value + y_in[half, shift].astype(F32)
        batch_sum.append(value.astype(BF16))

    def batch_out(i, carry):
        cols = pl.ds(pl.multiple_of(i * 256, 256), 256)
        value = dot_nt(batch_sum[0], proj[cols, 0:HD]) + dot_nt(batch_sum[1], proj[cols, HD:D])
        bg_out[:, cols] = value.astype(BF16)
        return carry

    lax.fori_loop(0, 4, batch_out, 0)

    for direction in (0, 1):
        rs(direction, 5).wait_recv()
        rs(direction, 6).wait_recv()
    for half in (0, 1):
        rows = slice(half * SUB, (half + 1) * SUB)
        value = gterm[rows, :] + t_buf[0, rows, :]
        value = value + (rs_in[half, 6].astype(F32) + rs_in[1 - half, 5].astype(F32))
        qg_out[rows, :] = (value * SCALE).astype(BF16)

    for direction in (0, 1):
        for n in range(7):
            ag(direction, n).wait_send()
            rs(direction, n).wait_send()
        for n in range(3):
            for half in (0, 1):
                xa(half, direction, n).wait_send()
                xr(half, direction, n).wait_send()
    small_wait(ids_in, one_s.at[0])
    small_wait(hs_in, one_s.at[1])
    small_wait(d_in, one_s.at[3])
    for half in (0, 1):
        all_wait(column.at[half, pl.ds(0, (NY - 1) * IB)], one_s.at[9 + half])
        all_wait(y_in.at[half, pl.ds(1, NY - 1)], one_s.at[5 + half])
    pool_swap.wait_send()
    g_swap.wait_send()


def shards(queries, batch_hidden, pool_hidden, projection, hard_ids, query_group, labels, group_lists):
    hbm = pl.BlockSpec(memory_space=pl.ANY)
    vmem = pl.BlockSpec(memory_space=pltpu.VMEM)
    dma = pltpu.SemaphoreType.DMA
    scratch = [
        pltpu.VMEM((NZ, QD, D), BF16),
        pltpu.VMEM((D, D), BF16),
        pltpu.VMEM((IB, D), BF16),
        pltpu.VMEM((PD, D), BF16),
        pltpu.VMEM((2 * PD, D), BF16),
        pltpu.VMEM((2, NB, HD), BF16),
        pltpu.VMEM((2 * PD, NZ * QD), BF16),
        pltpu.VMEM((NB, QD), F32),
        pltpu.VMEM((NB, QD), F32),
        pltpu.VMEM((GS, QD), jnp.int32),
        pltpu.VMEM((NZ, 2, QD), jnp.int32),
        pltpu.VMEM((NZ, 2, QD), jnp.int32),
        pltpu.VMEM((NZ, 2, QD), F32),
        pltpu.VMEM((NZ, 2, QD), F32),
        pltpu.VMEM((NZ, 2, QD), F32),
        pltpu.VMEM((NZ, 2, QD), F32),
        pltpu.VMEM((HN, QD), F32),
        pltpu.VMEM((QD, HN), jnp.int32),
        pltpu.VMEM((QD, HN), F32),
        pltpu.VMEM((NZ, QD, D), F32),
        pltpu.VMEM((2 * QD, 2 * PD), BF16),
        pltpu.VMEM((2, 7, SUB, D), BF16),
        pltpu.VMEM((2, 7, SUB, D), BF16),
        pltpu.VMEM((NB, QD), BF16),
        pltpu.VMEM((2, NB, HD), F32),
        pltpu.VMEM((2, 2, 3, SLAB // 2, HD), BF16),
        pltpu.VMEM((2, 2, 3, SLAB // 2, HD), BF16),
        pltpu.VMEM((2, NY, IB, HD), F32),
        pltpu.VMEM((2, NY, IB, HD), BF16),
        pltpu.VMEM((2, NY, IB, HD), BF16),
        pltpu.VMEM((QD, D), F32),
        pltpu.VMEM((2, NZ * QD, D), BF16),
        pltpu.VMEM((PD, D), F32),
        pltpu.VMEM((PD, D), F32),
        pltpu.VMEM((PD, D), F32),
        pltpu.VMEM((PD, D), BF16),
        dma((4,)),
        dma((2, 7)),
        dma((2, 7)),
        dma((2, 7)),
        dma((2, 7)),
        dma((2, 2, 3)),
        dma((2, 2, 3)),
        dma((2, 2, 3)),
        dma((2, 2, 3)),
        dma((11,)),
        dma((11,)),
        pltpu.SemaphoreType.REGULAR,
        pltpu.SemaphoreType.REGULAR,
    ]
    shapes = (
        pltpu.VMEM((QD, D), BF16),
        pltpu.VMEM((IB, D), BF16),
        pltpu.VMEM((PD, D), BF16),
    )
    return pl.pallas_call(
        kernel,
        out_shape=shapes,
        in_specs=[hbm] * 4 + [vmem] * 4,
        out_specs=(vmem, vmem, vmem),
        scratch_shapes=scratch,
        compiler_params=pltpu.CompilerParams(
            collective_id=0, has_side_effects=True, vmem_limit_bytes=58 * 1024 * 1024
        ),
        cost_estimate=pl.CostEstimate(flops=9_000_000_000, bytes_accessed=6_000_000, transcendentals=100_000),
    )(
        queries, batch_hidden, pool_hidden, projection, hard_ids.T,
        query_group.reshape(1, QD), labels.reshape(1, QD), group_lists,
    )


def solution(mesh):
    return jax.shard_map(
        shards,
        mesh=mesh,
        in_specs=(
            P(("pa", "pb"), None),
            P(("pa", "pb"), None),
            P(("pa", "pb"), None),
            P(),
            P(("pa", "pb"), None),
            P(("pa", "pb")),
            P(("pa", "pb")),
            P(),
        ),
        out_specs=(P(("pa", "pb"), None), P(("pa", "pb"), None), P(("pa", "pb"), None)),
        check_vma=False,
    )
```

```python
import math

import jax
import jax.numpy as jnp
from jax import lax
from jax.experimental import pallas as pl
from jax.experimental.pallas import tpu as pltpu
from jax.sharding import PartitionSpec as P

MESH = pl.DeviceIdType.MESH
NX, NY, NZ = 4, 8, 8
D = 1024
QD = 128
PD = 512
IB = 16
NG = 64
GS = 64
HN = 16
NB = NX * NY * IB
SLAB = NY * IB
SUB = QD // 2
HD = D // 2
SCALE = 1.0 / math.sqrt(D)
F32 = jnp.float32
BF16 = jnp.bfloat16
LOW = -3.0e38

MIRROR = (0, 1, 3, 2, 5, 4, 7, 6)


def slot_of(direction, hops):
    if hops == 0:
        return 0
    if hops == 4:
        return 1
    return 2 * hops + direction


def slot_shift(slot):
    if slot < 2:
        return 4 * slot
    hops = slot // 2
    return (hops if slot % 2 else -hops) % NZ


def dot(a, b):
    return jnp.dot(a, b, preferred_element_type=F32)


def dot_nt(a, b):
    return lax.dot_general(a, b, (((1,), (1,)), ((), ())), preferred_element_type=F32)


def eye(n):
    same = lax.broadcasted_iota(jnp.int32, (n, n), 0) == lax.broadcasted_iota(jnp.int32, (n, n), 1)
    return jnp.where(same, 1.0, 0.0).astype(BF16)


def turn_rows(rows):
    high = jnp.floor(rows * (1.0 / 32.0))
    low = rows - high * 32.0
    one = eye(QD)
    turned = dot_nt(one, high.astype(BF16)) * 32.0 + dot_nt(one, low.astype(BF16))
    return turned.astype(jnp.int32)


def kernel(
    q_hbm, bh_hbm, ph_hbm, proj_hbm, ids_ref, group_ref, label_ref, lists_ref,
    qg_out, bg_out, pg_out,
    qbuf, proj, bh, ph, pool, column, ot, mask, dense, chosen,
    ids_byz, ids_in, hs_out, hs_in, d_out, d_in, w_out, w_in, rows16, idcol, dcol, wcol, fcol,
    t_buf, o_buf, rs_out, rs_in, dg, part, xr_out, xr_in, xsum, y_out, y_in, gterm,
    contrib, g_send, g_recv, g_own, gb,
    ld_sem, ag_s, ag_r, rs_s, rs_r, xa_s, xa_r, xr_s, xr_r, one_s, one_r, z_ready, xy_ready,
):
    pa = lax.axis_index("pa")
    pb = lax.axis_index("pb")
    x, y = pa // NY, pa % NY
    z, core = pb // 2, pb % 2

    def at_z(shift):
        return (pa, ((z + shift + NZ) % NZ) * 2 + core)

    def at_y(shift):
        return (x * NY + (y + shift) % NY, pb)

    def at_x(shift):
        return (((x + shift + NX) % NX) * NY + y, pb)

    partner = (pa, z * 2 + 1 - core)

    def remote(src, dst, send, recv, device):
        return pltpu.make_async_remote_copy(
            src_ref=src, dst_ref=dst, send_sem=send, recv_sem=recv, device_id=device, device_id_type=MESH
        )

    barrier = pltpu.get_barrier_semaphore()

    def hello(device):
        pl.semaphore_signal(barrier, inc=1, device_id=device, device_id_type=MESH)

    for shift in range(1, NZ):
        hello((pa, ((z + shift) % NZ) * 2))
    hello(partner)
    for shift in range(1, NY):
        hello((x * NY + (y + shift) % NY, z * 2 + 1))
    for shift in (1, NX - 1):
        hello((((x + shift) % NX) * NY + y, z * 2 + 1))

    loads = [
        pltpu.make_async_copy(q_hbm, qbuf.at[0], ld_sem.at[0]),
        pltpu.make_async_copy(bh_hbm, bh, ld_sem.at[1]),
        pltpu.make_async_copy(proj_hbm, proj, ld_sem.at[2]),
        pltpu.make_async_copy(ph_hbm, ph, ld_sem.at[3]),
    ]
    for load in loads:
        load.start()
    loads[0].wait()

    @pl.when(core == 0)
    def _():
        pl.semaphore_wait(barrier, 2 * (NZ - 1) + 1)
        pl.semaphore_signal(z_ready, inc=1, device_id=partner, device_id_type=MESH)

    @pl.when(core == 1)
    def _():
        pl.semaphore_wait(z_ready, 1)

    def ag(direction, n):
        hops = n // 2
        rows = pl.ds((direction if n % 2 == 0 else 1 - direction) * SUB, SUB)
        return remote(
            qbuf.at[slot_of(direction, hops), rows],
            qbuf.at[slot_of(direction, hops + 1), rows],
            ag_s.at[direction, n],
            ag_r.at[direction, n],
            at_z(1 if direction == 0 else -1),
        )

    def ag_arrive(n):
        for direction in (0, 1):
            ag(direction, n).wait_recv()
            if n + 2 <= 6:
                ag(direction, n + 2).start()

    for n in (0, 1):
        for direction in (0, 1):
            ag(direction, n).start()

    def small(src, dst, which, slot):
        return remote(src, dst.at[MIRROR[slot]], one_s.at[which], one_r.at[which], at_z(slot_shift(slot)))

    def small_wait(buf, sem):
        pltpu.make_async_copy(buf.at[pl.ds(1, NZ - 1)], buf.at[pl.ds(1, NZ - 1)], sem).wait()

    loads[1].wait()
    loads[2].wait()
    own_rows = pl.ds(pl.multiple_of(pa * IB, IB), IB)

    def batch_half(half):
        def tile(i, carry):
            cols = pl.ds(pl.multiple_of(i * 256, 256), 256)
            wide = pl.ds(pl.multiple_of(half * HD + i * 256, 256), 256)
            column[half, own_rows, cols] = dot(bh[...], proj[:, wide]).astype(BF16)
            return carry

        lax.fori_loop(0, 2, tile, 0)

    def ya_send(half):
        here = column.at[half, own_rows]
        for shift in range(1, NY):
            remote(here, here, one_s.at[9 + half], one_r.at[9 + half], at_y(shift)).start()

    batch_half(0)

    @pl.when(core == 1)
    def _():
        pl.semaphore_wait(barrier, 2 * (NY - 1) + 2 * 2 + 1)
        pl.semaphore_signal(xy_ready, inc=1, device_id=partner, device_id_type=MESH)

    @pl.when(core == 0)
    def _():
        pl.semaphore_wait(xy_ready, 1)

    ya_send(0)
    batch_half(1)
    ya_send(1)

    local_rows = ids_ref[...] - lax.broadcasted_iota(jnp.int32, (HN, QD), 0) * PD
    for owner_z in range(NZ):
        ids_byz[owner_z] = local_rows[2 * owner_z : 2 * owner_z + 2, :]
    ids_in[0] = ids_byz[z]
    for slot in range(1, NZ):
        small(ids_byz.at[(z + slot_shift(slot)) % NZ], ids_in, 0, slot).start()

    ag_arrive(0)
    loads[3].wait()
    pool_rows = pl.ds(pl.multiple_of(core * PD, PD), PD)

    def pool_tile(i, carry):
        cols = pl.ds(pl.multiple_of(i * 256, 256), 256)
        pool[pool_rows, cols] = dot(ph[...], proj[:, cols]).astype(BF16)
        return carry

    lax.fori_loop(0, 4, pool_tile, 0)
    pool_swap = remote(pool.at[pool_rows], pool.at[pool_rows], one_s.at[7], one_r.at[7], partner)
    pool_swap.start()
    ag_arrive(1)

    lists_turned = lists_ref[...]
    high = (lists_turned // 32).astype(F32).astype(BF16)
    low = (lists_turned % 32).astype(F32).astype(BF16)
    one = eye(NG)
    high = dot_nt(one, high).astype(BF16)
    low = dot_nt(one, low).astype(BF16)
    in_group = lax.broadcasted_iota(jnp.int32, (NG, QD), 0) == group_ref[...]
    in_group = jnp.where(in_group, 1.0, 0.0).astype(BF16)
    chosen[...] = (dot(high, in_group) * 32.0 + dot(low, in_group)).astype(jnp.int32)
    at_label = lax.broadcasted_iota(jnp.int32, (GS, QD), 0) == label_ref[...]
    label_row = jnp.sum(jnp.where(at_label, chosen[...], 0), axis=0, keepdims=True)

    def mask_tile(i, carry):
        base = pl.multiple_of(i * 64, 64)
        row = lax.broadcasted_iota(jnp.int32, (64, QD), 0) + base
        found = jnp.zeros((64, QD), F32)
        for c in range(GS):
            found = jnp.where(row == chosen[c : c + 1, :], 1.0, found)
        mask[pl.ds(base, 64), :] = found
        return carry

    def slab(shift, half):
        start = ((x + shift + NX) % NX) * SLAB + half * (SLAB // 2)
        return pl.ds(pl.multiple_of(start, SLAB // 2), SLAB // 2)

    def xa(part_of, direction, n):
        half = direction if n % 2 == 0 else 1 - direction
        sign = 1 if direction == 0 else -1
        here = column.at[part_of, slab(0 if n < 2 else -sign, half)]
        return remote(here, here, xa_s.at[part_of, direction, n], xa_r.at[part_of, direction, n], at_x(sign))

    def all_wait(buf, sem):
        pltpu.make_async_copy(buf, buf, sem).wait()

    def xa_send(part_of):
        all_wait(column.at[part_of, pl.ds(0, (NY - 1) * IB)], one_r.at[9 + part_of])
        for n in (0, 1):
            for direction in (0, 1):
                xa(part_of, direction, n).start()

    def xa_arrive(part_of, n):
        for direction in (0, 1):
            xa(part_of, direction, n).wait_recv()
            if n == 0:
                xa(part_of, direction, 2).start()

    xa_send(0)
    lax.fori_loop(0, NB // 128, mask_tile, 0)
    ag_arrive(2)
    xa_send(1)
    small_wait(ids_in, one_r.at[0])
    for slot in range(NZ):
        rows16[2 * slot : 2 * slot + 2, :] = ids_in[slot].astype(F32)
    idcol[...] = turn_rows(rows16[...])
    pool_swap.wait_recv()

    def score(slot):
        queries = qbuf[slot : slot + 2].reshape(2 * QD, D)
        for k in (0, 1):

            def tile(i, carry):
                base = pl.multiple_of(i * 256, 256)
                rows = pl.ds(pl.multiple_of(k * PD + base, 256), 256)
                scores = dot_nt(pool[rows, :], queries)
                iota = lax.broadcasted_iota(jnp.int32, (256, QD), 0) + base
                new = []
                for j in (0, 1):
                    hit = iota == ids_in[slot + j, k : k + 1, :]
                    ot[rows, (slot + j) * QD : (slot + j + 1) * QD] = jnp.where(hit, 1.0, 0.0).astype(BF16)
                    found = jnp.where(hit, scores[:, j * QD : (j + 1) * QD], 0.0)
                    new.append(carry[j] + jnp.sum(found, axis=0, keepdims=True))
                return tuple(new)

            sums = lax.fori_loop(0, 2, tile, tuple(jnp.zeros((1, QD), F32) for _ in (0, 1)))
            for j in (0, 1):
                target = hs_in if slot + j == 0 else hs_out
                target[slot + j, k : k + 1, :] = sums[j] * SCALE
        for j in (0, 1):
            if slot + j > 0:
                small(hs_out.at[slot + j], hs_in, 1, slot + j).start()

    def dense_half(half):
        def tile(i, carry):
            rows = pl.ds(pl.multiple_of(i * 256, 256), 256)
            value = dot_nt(column[half, rows, :], qbuf[0, :, half * HD : (half + 1) * HD])
            if half == 0:
                dense[rows, :] = value
            else:
                value = (dense[rows, :] + value) * SCALE
                dense[rows, :] = jnp.where(mask[rows, :] > 0.0, value, LOW)
            return carry

        lax.fori_loop(0, NB // 256, tile, 0)

    score(2)
    ag_arrive(3)
    xa_arrive(0, 0)
    score(4)
    ag_arrive(4)
    lax.fori_loop(NB // 128, NB // 64, mask_tile, 0)
    xa_arrive(1, 0)
    ag_arrive(5)
    score(6)
    ag_arrive(6)
    score(0)

    small_wait(hs_in, one_r.at[1])
    hard = hs_in[...]
    hard_top = jnp.max(jnp.max(hard, axis=0), axis=0, keepdims=True)
    hard = jnp.exp(hard - hard_top[None])
    hard_sum = jnp.sum(jnp.sum(hard, axis=0), axis=0, keepdims=True)
    share = (hard / hard_sum[None]).astype(BF16).astype(F32)
    w_out[...] = share
    w_in[0] = share[0]
    for slot in range(1, NZ):
        small(w_out.at[slot], w_in, 2, slot).start()
    xa_arrive(0, 1)
    xa_arrive(0, 2)
    dense_half(0)

    def rs(direction, n):
        return remote(
            rs_out.at[direction, n],
            rs_in.at[direction, n],
            rs_s.at[direction, n],
            rs_r.at[direction, n],
            at_z(1 if direction == 0 else -1),
        )

    def rs_send(n):
        hops = 4 - (n + 1) // 2
        for direction in (0, 1):
            half = direction if n % 2 == 0 else 1 - direction
            value = t_buf[slot_of(1 - direction, hops), half * SUB : (half + 1) * SUB, :]
            if n >= 2:
                rs(direction, n - 2).wait_recv()
                value = value + rs_in[direction, n - 2].astype(F32)
            rs_out[direction, n] = value.astype(BF16)
            rs(direction, n).start()

    def terms(slot):
        lane = lax.broadcasted_iota(jnp.int32, (QD, PD), 1)
        for j in (0, 1):
            for k in (0, 1):
                at = 2 * (slot + j) + k
                hit = lane == idcol[:, at : at + 1]
                value = jnp.where(hit, wcol[:, at : at + 1], 0.0)
                o_buf[j * QD : (j + 1) * QD, k * PD : (k + 1) * PD] = value.astype(BF16)

        def tile(i, carry):
            cols = pl.ds(pl.multiple_of(i * 256, 256), 256)
            value = dot(o_buf[...], pool[:, cols])
            t_buf[slot, :, cols] = value[0:QD]
            t_buf[slot + 1, :, cols] = value[QD : 2 * QD]
            return carry

        lax.fori_loop(0, 4, tile, 0)

    def part_half(half):
        def tile(i, carry):
            cols = pl.ds(pl.multiple_of(i * 256, 256), 256)
            wide = pl.ds(pl.multiple_of(half * HD + i * 256, 256), 256)
            part[half, :, cols] = dot(dg[...], qbuf[0, :, wide]) * SCALE
            return carry

        lax.fori_loop(0, 2, tile, 0)

    def xr(part_of, direction, n):
        return remote(
            xr_out.at[part_of, direction, n],
            xr_in.at[part_of, direction, n],
            xr_s.at[part_of, direction, n],
            xr_r.at[part_of, direction, n],
            at_x(1 if direction == 0 else -1),
        )

    def xr_send(part_of, n):
        for direction in (0, 1):
            half = direction if n % 2 == 0 else 1 - direction
            sign = 1 if direction == 0 else -1
            value = part[part_of, slab(2 if n == 0 else sign, half), :]
            if n == 2:
                xr(part_of, direction, 0).wait_recv()
                value = value + xr_in[part_of, direction, 0].astype(F32)
            xr_out[part_of, direction, n] = value.astype(BF16)
            xr(part_of, direction, n).start()

    def yr_send(part_of):
        for direction in (0, 1):
            xr(part_of, direction, 1).wait_recv()
            xr(part_of, direction, 2).wait_recv()
        for half in (0, 1):
            value = part[part_of, slab(0, half), :]
            value = value + xr_in[part_of, half, 2].astype(F32) + xr_in[part_of, 1 - half, 1].astype(F32)
            xsum[part_of, half * 4 : half * 4 + 4] = value.reshape(NY // 2, IB, HD)
            y_out[part_of, half * 4 : half * 4 + 4] = value.astype(BF16).reshape(NY // 2, IB, HD)
        for shift in range(1, NY):
            remote(
                y_out.at[part_of, (y + shift) % NY],
                y_in.at[part_of, shift],
                one_s.at[5 + part_of],
                one_r.at[5 + part_of],
                at_y(shift),
            ).start()

    def contribs(which):
        k = 1 - core if which == 0 else core
        for slot in range(NZ):
            at = 2 * slot
            weight = jnp.where(k == 0, dcol[:, at : at + 1], dcol[:, at + 1 : at + 2]) * SCALE
            contrib[which, slot * QD : (slot + 1) * QD, :] = (qbuf[slot].astype(F32) * weight).astype(BF16)

    def pool_sum(which, target, first, last):
        k = 1 - core if which == 0 else core

        def tile(i, carry):
            cols = pl.ds(pl.multiple_of(i * 256, 256), 256)
            target[:, cols] = dot(ot[pl.ds(pl.multiple_of(k * PD, PD), PD), :], contrib[which, :, cols])
            return carry

        lax.fori_loop(first, last, tile, 0)

    def group_term():
        dg_turned = dot_nt(eye(QD), dg[...]).astype(BF16)
        for half in (0, 1):

            def tile(i, carry):
                cols = pl.ds(pl.multiple_of(i * 256, 256), 256)
                wide = pl.ds(pl.multiple_of(half * HD + i * 256, 256), 256)
                gterm[:, wide] = dot(dg_turned, column[half, :, cols])
                return carry

            lax.fori_loop(0, 2, tile, 0)

    small_wait(w_in, one_r.at[2])
    for slot in range(NZ):
        rows16[2 * slot : 2 * slot + 2, :] = w_in[slot]
    wcol[...] = dot_nt(eye(QD), rows16[...].astype(BF16))
    terms(0)
    rs_send(0)
    terms(6)
    rs_send(1)
    xa_arrive(1, 1)
    xa_arrive(1, 2)
    dense_half(1)

    group_max = jnp.max(dense[...], axis=0, keepdims=True)
    top = jnp.maximum(group_max, hard_top)
    hard = jnp.exp(hs_in[...] - top[None])
    likely = jnp.where(mask[...] > 0.0, jnp.exp(dense[...] - top), 0.0)
    total = jnp.sum(likely, axis=0, keepdims=True) + jnp.sum(jnp.sum(hard, axis=0), axis=0, keepdims=True)
    factor = hard_sum * jnp.exp(hard_top - top) / total
    here = lax.broadcasted_iota(jnp.int32, (QD, QD), 0) == lax.broadcasted_iota(jnp.int32, (QD, QD), 1)
    fcol[...] = jnp.sum(jnp.where(here, factor, 0.0), axis=1, keepdims=True)
    d_hard = (hard / total[None]).astype(BF16).astype(F32)
    d_out[...] = d_hard
    d_in[0] = d_hard[0]
    for slot in range(1, NZ):
        small(d_out.at[slot], d_in, 3, slot).start()
    target = jnp.where(lax.broadcasted_iota(jnp.int32, (NB, QD), 0) == label_row, 1.0, 0.0)
    dg[...] = (likely / total - target).astype(BF16)

    part_half(0)
    xr_send(0, 0)
    xr_send(0, 1)
    part_half(1)
    xr_send(1, 0)
    xr_send(1, 1)
    terms(4)
    rs_send(2)
    terms(2)
    xr_send(0, 2)
    rs_send(3)
    xr_send(1, 2)
    small_wait(d_in, one_r.at[3])
    for slot in range(NZ):
        rows16[2 * slot : 2 * slot + 2, :] = d_in[slot]
    dcol[...] = dot_nt(eye(QD), rows16[...].astype(BF16))
    contribs(0)
    rs_send(4)
    pool_sum(0, g_send, 0, 4)
    g_swap = remote(g_send, g_recv, one_s.at[8], one_r.at[8], partner)
    g_swap.start()
    yr_send(0)
    rs_send(5)
    yr_send(1)
    rs_send(6)
    contribs(1)
    pool_sum(1, g_own, 0, 4)
    group_term()
    g_swap.wait_recv()
    gb[...] = (g_own[...] + g_recv[...]).astype(BF16)

    def pool_out(i, carry):
        cols = pl.ds(pl.multiple_of(i * 256, 256), 256)
        pg_out[:, cols] = dot_nt(gb[...], proj[cols, :]).astype(BF16)
        return carry

    lax.fori_loop(0, 4, pool_out, 0)

    batch_sum = []
    for half in (0, 1):
        all_wait(y_in.at[half, pl.ds(1, NY - 1)], one_r.at[5 + half])
        value = xsum[half, y]
        for shift in range(1, NY):
            value = value + y_in[half, shift].astype(F32)
        batch_sum.append(value.astype(BF16))

    def batch_out(i, carry):
        cols = pl.ds(pl.multiple_of(i * 256, 256), 256)
        value = dot_nt(batch_sum[0], proj[cols, 0:HD]) + dot_nt(batch_sum[1], proj[cols, HD:D])
        bg_out[:, cols] = value.astype(BF16)
        return carry

    lax.fori_loop(0, 4, batch_out, 0)

    for direction in (0, 1):
        rs(direction, 5).wait_recv()
        rs(direction, 6).wait_recv()
    for half in (0, 1):
        rows = slice(half * SUB, (half + 1) * SUB)
        value = t_buf[0, rows, :] + (rs_in[half, 6].astype(F32) + rs_in[1 - half, 5].astype(F32))
        value = gterm[rows, :] + value * fcol[rows, :]
        qg_out[rows, :] = (value * SCALE).astype(BF16)

    for direction in (0, 1):
        for n in range(7):
            ag(direction, n).wait_send()
            rs(direction, n).wait_send()
        for n in range(3):
            for half in (0, 1):
                xa(half, direction, n).wait_send()
                xr(half, direction, n).wait_send()
    small_wait(ids_in, one_s.at[0])
    small_wait(hs_in, one_s.at[1])
    small_wait(w_in, one_s.at[2])
    small_wait(d_in, one_s.at[3])
    for half in (0, 1):
        all_wait(column.at[half, pl.ds(0, (NY - 1) * IB)], one_s.at[9 + half])
        all_wait(y_in.at[half, pl.ds(1, NY - 1)], one_s.at[5 + half])
    pool_swap.wait_send()
    g_swap.wait_send()


def shards(queries, batch_hidden, pool_hidden, projection, hard_ids, query_group, labels, group_lists):
    hbm = pl.BlockSpec(memory_space=pl.ANY)
    vmem = pl.BlockSpec(memory_space=pltpu.VMEM)
    dma = pltpu.SemaphoreType.DMA
    scratch = [
        pltpu.VMEM((NZ, QD, D), BF16),
        pltpu.VMEM((D, D), BF16),
        pltpu.VMEM((IB, D), BF16),
        pltpu.VMEM((PD, D), BF16),
        pltpu.VMEM((2 * PD, D), BF16),
        pltpu.VMEM((2, NB, HD), BF16),
        pltpu.VMEM((2 * PD, NZ * QD), BF16),
        pltpu.VMEM((NB, QD), F32),
        pltpu.VMEM((NB, QD), F32),
        pltpu.VMEM((GS, QD), jnp.int32),
        pltpu.VMEM((NZ, 2, QD), jnp.int32),
        pltpu.VMEM((NZ, 2, QD), jnp.int32),
        pltpu.VMEM((NZ, 2, QD), F32),
        pltpu.VMEM((NZ, 2, QD), F32),
        pltpu.VMEM((NZ, 2, QD), F32),
        pltpu.VMEM((NZ, 2, QD), F32),
        pltpu.VMEM((NZ, 2, QD), F32),
        pltpu.VMEM((NZ, 2, QD), F32),
        pltpu.VMEM((HN, QD), F32),
        pltpu.VMEM((QD, HN), jnp.int32),
        pltpu.VMEM((QD, HN), F32),
        pltpu.VMEM((QD, HN), F32),
        pltpu.VMEM((QD, 1), F32),
        pltpu.VMEM((NZ, QD, D), F32),
        pltpu.VMEM((2 * QD, 2 * PD), BF16),
        pltpu.VMEM((2, 7, SUB, D), BF16),
        pltpu.VMEM((2, 7, SUB, D), BF16),
        pltpu.VMEM((NB, QD), BF16),
        pltpu.VMEM((2, NB, HD), F32),
        pltpu.VMEM((2, 2, 3, SLAB // 2, HD), BF16),
        pltpu.VMEM((2, 2, 3, SLAB // 2, HD), BF16),
        pltpu.VMEM((2, NY, IB, HD), F32),
        pltpu.VMEM((2, NY, IB, HD), BF16),
        pltpu.VMEM((2, NY, IB, HD), BF16),
        pltpu.VMEM((QD, D), F32),
        pltpu.VMEM((2, NZ * QD, D), BF16),
        pltpu.VMEM((PD, D), F32),
        pltpu.VMEM((PD, D), F32),
        pltpu.VMEM((PD, D), F32),
        pltpu.VMEM((PD, D), BF16),
        dma((4,)),
        dma((2, 7)),
        dma((2, 7)),
        dma((2, 7)),
        dma((2, 7)),
        dma((2, 2, 3)),
        dma((2, 2, 3)),
        dma((2, 2, 3)),
        dma((2, 2, 3)),
        dma((11,)),
        dma((11,)),
        pltpu.SemaphoreType.REGULAR,
        pltpu.SemaphoreType.REGULAR,
    ]
    shapes = (
        pltpu.VMEM((QD, D), BF16),
        pltpu.VMEM((IB, D), BF16),
        pltpu.VMEM((PD, D), BF16),
    )
    return pl.pallas_call(
        kernel,
        out_shape=shapes,
        in_specs=[hbm] * 4 + [vmem] * 4,
        out_specs=(vmem, vmem, vmem),
        scratch_shapes=scratch,
        compiler_params=pltpu.CompilerParams(
            collective_id=0, has_side_effects=True, vmem_limit_bytes=58 * 1024 * 1024
        ),
        cost_estimate=pl.CostEstimate(flops=9_000_000_000, bytes_accessed=6_000_000, transcendentals=100_000),
    )(
        queries, batch_hidden, pool_hidden, projection, hard_ids.T,
        query_group.reshape(1, QD), labels.reshape(1, QD), group_lists,
    )


def solution(mesh):
    return jax.shard_map(
        shards,
        mesh=mesh,
        in_specs=(
            P(("pa", "pb"), None),
            P(("pa", "pb"), None),
            P(("pa", "pb"), None),
            P(),
            P(("pa", "pb"), None),
            P(("pa", "pb")),
            P(("pa", "pb")),
            P(),
        ),
        out_specs=(P(("pa", "pb"), None), P(("pa", "pb"), None), P(("pa", "pb"), None)),
        check_vma=False,
    )
```

```python
import math

import jax
import jax.numpy as jnp
from jax import lax
from jax.experimental import pallas as pl
from jax.experimental.pallas import tpu as pltpu
from jax.sharding import PartitionSpec as P

MESH = pl.DeviceIdType.MESH
NX, NY, NZ = 4, 8, 8
D = 1024
QD = 128
PD = 512
IB = 16
NG = 64
GS = 64
HN = 16
NB = NX * NY * IB
SLAB = NY * IB
SUB = QD // 2
HD = D // 2
SCALE = 1.0 / math.sqrt(D)
F32 = jnp.float32
BF16 = jnp.bfloat16
LOW = -3.0e38

MIRROR = (0, 1, 3, 2, 5, 4, 7, 6)


def slot_of(direction, hops):
    if hops == 0:
        return 0
    if hops == 4:
        return 1
    return 2 * hops + direction


def slot_shift(slot):
    if slot < 2:
        return 4 * slot
    hops = slot // 2
    return (hops if slot % 2 else -hops) % NZ


def dot(a, b):
    return jnp.dot(a, b, preferred_element_type=F32)


def dot_nt(a, b):
    return lax.dot_general(a, b, (((1,), (1,)), ((), ())), preferred_element_type=F32)


def eye(n):
    same = lax.broadcasted_iota(jnp.int32, (n, n), 0) == lax.broadcasted_iota(jnp.int32, (n, n), 1)
    return jnp.where(same, 1.0, 0.0).astype(BF16)


def turn_rows(rows):
    high = jnp.floor(rows * (1.0 / 32.0))
    low = rows - high * 32.0
    one = eye(QD)
    turned = dot_nt(one, high.astype(BF16)) * 32.0 + dot_nt(one, low.astype(BF16))
    return turned.astype(jnp.int32)


def kernel(
    q_hbm, bh_hbm, ph_hbm, proj_hbm, ids_ref, group_ref, label_ref, lists_ref,
    qg_out, bg_out, pg_out,
    qbuf, proj, bh, ph, pool, column, ot, mask, dense, chosen,
    ids_byz, ids_in, hs_out, hs_in, d_out, d_in, w_out, w_in, rows16, idcol, dcol, wcol, fcol,
    t_buf, o_buf, rs_out, rs_in, dg, part, xr_out, xr_in, xsum, y_out, y_in, gterm,
    contrib, g_send, g_recv, g_own, gb,
    ld_sem, ag_s, ag_r, rs_s, rs_r, xa_s, xa_r, xr_s, xr_r, one_s, one_r, z_ready, xy_ready,
):
    pa = lax.axis_index("pa")
    pb = lax.axis_index("pb")
    x, y = pa // NY, pa % NY
    z, core = pb // 2, pb % 2

    def at_z(shift):
        return (pa, ((z + shift + NZ) % NZ) * 2 + core)

    def at_y(shift):
        return (x * NY + (y + shift) % NY, pb)

    def at_x(shift):
        return (((x + shift + NX) % NX) * NY + y, pb)

    partner = (pa, z * 2 + 1 - core)

    def remote(src, dst, send, recv, device):
        return pltpu.make_async_remote_copy(
            src_ref=src, dst_ref=dst, send_sem=send, recv_sem=recv, device_id=device, device_id_type=MESH
        )

    barrier = pltpu.get_barrier_semaphore()

    def hello(device):
        pl.semaphore_signal(barrier, inc=1, device_id=device, device_id_type=MESH)

    for shift in range(1, NZ):
        hello((pa, ((z + shift) % NZ) * 2))
    hello(partner)
    for shift in range(1, NY):
        hello((x * NY + (y + shift) % NY, z * 2 + 1))
    for shift in (1, NX - 1):
        hello((((x + shift) % NX) * NY + y, z * 2 + 1))

    loads = [
        pltpu.make_async_copy(q_hbm, qbuf.at[0], ld_sem.at[0]),
        pltpu.make_async_copy(bh_hbm, bh, ld_sem.at[1]),
        pltpu.make_async_copy(proj_hbm, proj, ld_sem.at[2]),
        pltpu.make_async_copy(ph_hbm, ph, ld_sem.at[3]),
    ]
    for load in loads:
        load.start()
    loads[0].wait()

    @pl.when(core == 0)
    def _():
        pl.semaphore_wait(barrier, 2 * (NZ - 1) + 1)
        pl.semaphore_signal(z_ready, inc=1, device_id=partner, device_id_type=MESH)

    @pl.when(core == 1)
    def _():
        pl.semaphore_wait(z_ready, 1)

    def ag(direction, n):
        hops = n // 2
        rows = pl.ds((direction if n % 2 == 0 else 1 - direction) * SUB, SUB)
        return remote(
            qbuf.at[slot_of(direction, hops), rows],
            qbuf.at[slot_of(direction, hops + 1), rows],
            ag_s.at[direction, n],
            ag_r.at[direction, n],
            at_z(1 if direction == 0 else -1),
        )

    def ag_arrive(n):
        for direction in (0, 1):
            ag(direction, n).wait_recv()
            if n + 2 <= 6:
                ag(direction, n + 2).start()

    for n in (0, 1):
        for direction in (0, 1):
            ag(direction, n).start()

    def small(src, dst, which, slot):
        return remote(src, dst.at[MIRROR[slot]], one_s.at[which], one_r.at[which], at_z(slot_shift(slot)))

    def small_wait(buf, sem):
        pltpu.make_async_copy(buf.at[pl.ds(1, NZ - 1)], buf.at[pl.ds(1, NZ - 1)], sem).wait()

    loads[1].wait()
    loads[2].wait()
    own_rows = pl.ds(pl.multiple_of(pa * IB, IB), IB)

    def batch_half(half):
        def tile(i, carry):
            cols = pl.ds(pl.multiple_of(i * 256, 256), 256)
            wide = pl.ds(pl.multiple_of(half * HD + i * 256, 256), 256)
            column[half, own_rows, cols] = dot(bh[...], proj[:, wide]).astype(BF16)
            return carry

        lax.fori_loop(0, 2, tile, 0)

    def ya_send(half):
        here = column.at[half, own_rows]
        for shift in range(1, NY):
            remote(here, here, one_s.at[9 + half], one_r.at[9 + half], at_y(shift)).start()

    batch_half(0)
    batch_half(1)

    local_rows = ids_ref[...] - lax.broadcasted_iota(jnp.int32, (HN, QD), 0) * PD
    for owner_z in range(NZ):
        ids_byz[owner_z] = local_rows[2 * owner_z : 2 * owner_z + 2, :]
    ids_in[0] = ids_byz[z]
    for slot in range(1, NZ):
        small(ids_byz.at[(z + slot_shift(slot)) % NZ], ids_in, 0, slot).start()

    ag_arrive(0)

    @pl.when(core == 1)
    def _():
        pl.semaphore_wait(barrier, 2 * (NY - 1) + 2 * 2 + 1)
        pl.semaphore_signal(xy_ready, inc=1, device_id=partner, device_id_type=MESH)

    @pl.when(core == 0)
    def _():
        pl.semaphore_wait(xy_ready, 1)

    ya_send(0)
    ya_send(1)

    loads[3].wait()
    pool_rows = pl.ds(pl.multiple_of(core * PD, PD), PD)

    def pool_tile(i, carry):
        cols = pl.ds(pl.multiple_of(i * 256, 256), 256)
        pool[pool_rows, cols] = dot(ph[...], proj[:, cols]).astype(BF16)
        return carry

    lax.fori_loop(0, 4, pool_tile, 0)
    pool_swap = remote(pool.at[pool_rows], pool.at[pool_rows], one_s.at[7], one_r.at[7], partner)
    pool_swap.start()
    ag_arrive(1)

    lists_turned = lists_ref[...]
    high = (lists_turned // 32).astype(F32).astype(BF16)
    low = (lists_turned % 32).astype(F32).astype(BF16)
    one = eye(NG)
    high = dot_nt(one, high).astype(BF16)
    low = dot_nt(one, low).astype(BF16)
    in_group = lax.broadcasted_iota(jnp.int32, (NG, QD), 0) == group_ref[...]
    in_group = jnp.where(in_group, 1.0, 0.0).astype(BF16)
    chosen[...] = (dot(high, in_group) * 32.0 + dot(low, in_group)).astype(jnp.int32)
    at_label = lax.broadcasted_iota(jnp.int32, (GS, QD), 0) == label_ref[...]
    label_row = jnp.sum(jnp.where(at_label, chosen[...], 0), axis=0, keepdims=True)

    def mask_tile(i, carry):
        base = pl.multiple_of(i * 64, 64)
        row = lax.broadcasted_iota(jnp.int32, (64, QD), 0) + base
        found = jnp.zeros((64, QD), F32)
        for c in range(GS):
            found = jnp.where(row == chosen[c : c + 1, :], 1.0, found)
        mask[pl.ds(base, 64), :] = found
        return carry

    def slab(shift, half):
        start = ((x + shift + NX) % NX) * SLAB + half * (SLAB // 2)
        return pl.ds(pl.multiple_of(start, SLAB // 2), SLAB // 2)

    def xa(part_of, direction, n):
        half = direction if n % 2 == 0 else 1 - direction
        sign = 1 if direction == 0 else -1
        here = column.at[part_of, slab(0 if n < 2 else -sign, half)]
        return remote(here, here, xa_s.at[part_of, direction, n], xa_r.at[part_of, direction, n], at_x(sign))

    def all_wait(buf, sem):
        pltpu.make_async_copy(buf, buf, sem).wait()

    def xa_send(part_of):
        all_wait(column.at[part_of, pl.ds(0, (NY - 1) * IB)], one_r.at[9 + part_of])
        for n in (0, 1):
            for direction in (0, 1):
                xa(part_of, direction, n).start()

    def xa_arrive(part_of, n):
        for direction in (0, 1):
            xa(part_of, direction, n).wait_recv()
            if n == 0:
                xa(part_of, direction, 2).start()

    lax.fori_loop(0, NB // 128, mask_tile, 0)
    ag_arrive(2)
    xa_send(0)
    small_wait(ids_in, one_r.at[0])
    for slot in range(NZ):
        rows16[2 * slot : 2 * slot + 2, :] = ids_in[slot].astype(F32)
    idcol[...] = turn_rows(rows16[...])
    pool_swap.wait_recv()

    def score(slot):
        queries = qbuf[slot : slot + 2].reshape(2 * QD, D)
        for k in (0, 1):

            def tile(i, carry):
                base = pl.multiple_of(i * 256, 256)
                rows = pl.ds(pl.multiple_of(k * PD + base, 256), 256)
                scores = dot_nt(pool[rows, :], queries)
                iota = lax.broadcasted_iota(jnp.int32, (256, QD), 0) + base
                new = []
                for j in (0, 1):
                    hit = iota == ids_in[slot + j, k : k + 1, :]
                    ot[rows, (slot + j) * QD : (slot + j + 1) * QD] = jnp.where(hit, 1.0, 0.0).astype(BF16)
                    found = jnp.where(hit, scores[:, j * QD : (j + 1) * QD], 0.0)
                    new.append(carry[j] + jnp.sum(found, axis=0, keepdims=True))
                return tuple(new)

            sums = lax.fori_loop(0, 2, tile, tuple(jnp.zeros((1, QD), F32) for _ in (0, 1)))
            for j in (0, 1):
                target = hs_in if slot + j == 0 else hs_out
                target[slot + j, k : k + 1, :] = sums[j] * SCALE
        for j in (0, 1):
            if slot + j > 0:
                small(hs_out.at[slot + j], hs_in, 1, slot + j).start()

    def dense_half(half):
        def tile(i, carry):
            rows = pl.ds(pl.multiple_of(i * 256, 256), 256)
            value = dot_nt(column[half, rows, :], qbuf[0, :, half * HD : (half + 1) * HD])
            if half == 0:
                dense[rows, :] = value
            else:
                value = (dense[rows, :] + value) * SCALE
                dense[rows, :] = jnp.where(mask[rows, :] > 0.0, value, LOW)
            return carry

        lax.fori_loop(0, NB // 256, tile, 0)

    score(2)
    ag_arrive(3)
    xa_send(1)
    score(4)
    ag_arrive(4)
    lax.fori_loop(NB // 128, NB // 64, mask_tile, 0)
    xa_arrive(0, 0)
    ag_arrive(5)
    score(6)
    xa_arrive(1, 0)
    ag_arrive(6)
    score(0)

    small_wait(hs_in, one_r.at[1])
    hard = hs_in[...]
    hard_top = jnp.max(jnp.max(hard, axis=0), axis=0, keepdims=True)
    hard = jnp.exp(hard - hard_top[None])
    hard_sum = jnp.sum(jnp.sum(hard, axis=0), axis=0, keepdims=True)
    share = (hard / hard_sum[None]).astype(BF16).astype(F32)
    w_out[...] = share
    w_in[0] = share[0]
    for slot in range(1, NZ):
        small(w_out.at[slot], w_in, 2, slot).start()
    xa_arrive(0, 1)
    xa_arrive(0, 2)
    dense_half(0)

    def rs(direction, n):
        return remote(
            rs_out.at[direction, n],
            rs_in.at[direction, n],
            rs_s.at[direction, n],
            rs_r.at[direction, n],
            at_z(1 if direction == 0 else -1),
        )

    def rs_send(n):
        hops = 4 - (n + 1) // 2
        for direction in (0, 1):
            half = direction if n % 2 == 0 else 1 - direction
            value = t_buf[slot_of(1 - direction, hops), half * SUB : (half + 1) * SUB, :]
            if n >= 2:
                rs(direction, n - 2).wait_recv()
                value = value + rs_in[direction, n - 2].astype(F32)
            rs_out[direction, n] = value.astype(BF16)
            rs(direction, n).start()

    def terms(slot):
        lane = lax.broadcasted_iota(jnp.int32, (QD, PD), 1)
        for j in (0, 1):
            for k in (0, 1):
                at = 2 * (slot + j) + k
                hit = lane == idcol[:, at : at + 1]
                value = jnp.where(hit, wcol[:, at : at + 1], 0.0)
                o_buf[j * QD : (j + 1) * QD, k * PD : (k + 1) * PD] = value.astype(BF16)

        def tile(i, carry):
            cols = pl.ds(pl.multiple_of(i * 256, 256), 256)
            value = dot(o_buf[...], pool[:, cols])
            t_buf[slot, :, cols] = value[0:QD]
            t_buf[slot + 1, :, cols] = value[QD : 2 * QD]
            return carry

        lax.fori_loop(0, 4, tile, 0)

    def part_half(half):
        def tile(i, carry):
            cols = pl.ds(pl.multiple_of(i * 256, 256), 256)
            wide = pl.ds(pl.multiple_of(half * HD + i * 256, 256), 256)
            part[half, :, cols] = dot(dg[...], qbuf[0, :, wide]) * SCALE
            return carry

        lax.fori_loop(0, 2, tile, 0)

    def xr(part_of, direction, n):
        return remote(
            xr_out.at[part_of, direction, n],
            xr_in.at[part_of, direction, n],
            xr_s.at[part_of, direction, n],
            xr_r.at[part_of, direction, n],
            at_x(1 if direction == 0 else -1),
        )

    def xr_send(part_of, n):
        for direction in (0, 1):
            half = direction if n % 2 == 0 else 1 - direction
            sign = 1 if direction == 0 else -1
            value = part[part_of, slab(2 if n == 0 else sign, half), :]
            if n == 2:
                xr(part_of, direction, 0).wait_recv()
                value = value + xr_in[part_of, direction, 0].astype(F32)
            xr_out[part_of, direction, n] = value.astype(BF16)
            xr(part_of, direction, n).start()

    def yr_send(part_of):
        for direction in (0, 1):
            xr(part_of, direction, 1).wait_recv()
            xr(part_of, direction, 2).wait_recv()
        for half in (0, 1):
            value = part[part_of, slab(0, half), :]
            value = value + xr_in[part_of, half, 2].astype(F32) + xr_in[part_of, 1 - half, 1].astype(F32)
            xsum[part_of, half * 4 : half * 4 + 4] = value.reshape(NY // 2, IB, HD)
            y_out[part_of, half * 4 : half * 4 + 4] = value.astype(BF16).reshape(NY // 2, IB, HD)
        for shift in range(1, NY):
            remote(
                y_out.at[part_of, (y + shift) % NY],
                y_in.at[part_of, shift],
                one_s.at[5 + part_of],
                one_r.at[5 + part_of],
                at_y(shift),
            ).start()

    def contribs(which):
        k = 1 - core if which == 0 else core
        for slot in range(NZ):
            at = 2 * slot
            weight = jnp.where(k == 0, dcol[:, at : at + 1], dcol[:, at + 1 : at + 2]) * SCALE
            contrib[which, slot * QD : (slot + 1) * QD, :] = (qbuf[slot].astype(F32) * weight).astype(BF16)

    def pool_sum(which, target, first, last):
        k = 1 - core if which == 0 else core

        def tile(i, carry):
            cols = pl.ds(pl.multiple_of(i * 256, 256), 256)
            target[:, cols] = dot(ot[pl.ds(pl.multiple_of(k * PD, PD), PD), :], contrib[which, :, cols])
            return carry

        lax.fori_loop(first, last, tile, 0)

    def group_term():
        dg_turned = dot_nt(eye(QD), dg[...]).astype(BF16)
        for half in (0, 1):

            def tile(i, carry):
                cols = pl.ds(pl.multiple_of(i * 256, 256), 256)
                wide = pl.ds(pl.multiple_of(half * HD + i * 256, 256), 256)
                gterm[:, wide] = dot(dg_turned, column[half, :, cols])
                return carry

            lax.fori_loop(0, 2, tile, 0)

    small_wait(w_in, one_r.at[2])
    for slot in range(NZ):
        rows16[2 * slot : 2 * slot + 2, :] = w_in[slot]
    wcol[...] = dot_nt(eye(QD), rows16[...].astype(BF16))
    terms(0)
    rs_send(0)
    terms(6)
    rs_send(1)
    xa_arrive(1, 1)
    xa_arrive(1, 2)
    dense_half(1)

    group_max = jnp.max(dense[...], axis=0, keepdims=True)
    top = jnp.maximum(group_max, hard_top)
    hard = jnp.exp(hs_in[...] - top[None])
    likely = jnp.where(mask[...] > 0.0, jnp.exp(dense[...] - top), 0.0)
    total = jnp.sum(likely, axis=0, keepdims=True) + jnp.sum(jnp.sum(hard, axis=0), axis=0, keepdims=True)
    factor = hard_sum * jnp.exp(hard_top - top) / total
    here = lax.broadcasted_iota(jnp.int32, (QD, QD), 0) == lax.broadcasted_iota(jnp.int32, (QD, QD), 1)
    fcol[...] = jnp.sum(jnp.where(here, factor, 0.0), axis=1, keepdims=True)
    d_hard = (hard / total[None]).astype(BF16).astype(F32)
    d_out[...] = d_hard
    d_in[0] = d_hard[0]
    for slot in range(1, NZ):
        small(d_out.at[slot], d_in, 3, slot).start()
    target = jnp.where(lax.broadcasted_iota(jnp.int32, (NB, QD), 0) == label_row, 1.0, 0.0)
    dg[...] = (likely / total - target).astype(BF16)

    part_half(0)
    xr_send(0, 0)
    xr_send(0, 1)
    part_half(1)
    xr_send(1, 0)
    xr_send(1, 1)
    terms(4)
    rs_send(2)
    terms(2)
    xr_send(0, 2)
    rs_send(3)
    xr_send(1, 2)
    small_wait(d_in, one_r.at[3])
    for slot in range(NZ):
        rows16[2 * slot : 2 * slot + 2, :] = d_in[slot]
    dcol[...] = dot_nt(eye(QD), rows16[...].astype(BF16))
    contribs(0)
    rs_send(4)
    pool_sum(0, g_send, 0, 4)
    g_swap = remote(g_send, g_recv, one_s.at[8], one_r.at[8], partner)
    g_swap.start()
    yr_send(0)
    rs_send(5)
    yr_send(1)
    rs_send(6)
    contribs(1)
    pool_sum(1, g_own, 0, 4)
    group_term()
    g_swap.wait_recv()
    gb[...] = (g_own[...] + g_recv[...]).astype(BF16)

    def pool_out(i, carry):
        cols = pl.ds(pl.multiple_of(i * 256, 256), 256)
        pg_out[:, cols] = dot_nt(gb[...], proj[cols, :]).astype(BF16)
        return carry

    lax.fori_loop(0, 4, pool_out, 0)

    batch_sum = []
    for half in (0, 1):
        all_wait(y_in.at[half, pl.ds(1, NY - 1)], one_r.at[5 + half])
        value = xsum[half, y]
        for shift in range(1, NY):
            value = value + y_in[half, shift].astype(F32)
        batch_sum.append(value.astype(BF16))

    def batch_out(i, carry):
        cols = pl.ds(pl.multiple_of(i * 256, 256), 256)
        value = dot_nt(batch_sum[0], proj[cols, 0:HD]) + dot_nt(batch_sum[1], proj[cols, HD:D])
        bg_out[:, cols] = value.astype(BF16)
        return carry

    lax.fori_loop(0, 4, batch_out, 0)

    for direction in (0, 1):
        rs(direction, 5).wait_recv()
        rs(direction, 6).wait_recv()
    for half in (0, 1):
        rows = slice(half * SUB, (half + 1) * SUB)
        value = t_buf[0, rows, :] + (rs_in[half, 6].astype(F32) + rs_in[1 - half, 5].astype(F32))
        value = gterm[rows, :] + value * fcol[rows, :]
        qg_out[rows, :] = (value * SCALE).astype(BF16)

    for direction in (0, 1):
        for n in range(7):
            ag(direction, n).wait_send()
            rs(direction, n).wait_send()
        for n in range(3):
            for half in (0, 1):
                xa(half, direction, n).wait_send()
                xr(half, direction, n).wait_send()
    small_wait(ids_in, one_s.at[0])
    small_wait(hs_in, one_s.at[1])
    small_wait(w_in, one_s.at[2])
    small_wait(d_in, one_s.at[3])
    for half in (0, 1):
        all_wait(column.at[half, pl.ds(0, (NY - 1) * IB)], one_s.at[9 + half])
        all_wait(y_in.at[half, pl.ds(1, NY - 1)], one_s.at[5 + half])
    pool_swap.wait_send()
    g_swap.wait_send()


def shards(queries, batch_hidden, pool_hidden, projection, hard_ids, query_group, labels, group_lists):
    hbm = pl.BlockSpec(memory_space=pl.ANY)
    vmem = pl.BlockSpec(memory_space=pltpu.VMEM)
    dma = pltpu.SemaphoreType.DMA
    scratch = [
        pltpu.VMEM((NZ, QD, D), BF16),
        pltpu.VMEM((D, D), BF16),
        pltpu.VMEM((IB, D), BF16),
        pltpu.VMEM((PD, D), BF16),
        pltpu.VMEM((2 * PD, D), BF16),
        pltpu.VMEM((2, NB, HD), BF16),
        pltpu.VMEM((2 * PD, NZ * QD), BF16),
        pltpu.VMEM((NB, QD), F32),
        pltpu.VMEM((NB, QD), F32),
        pltpu.VMEM((GS, QD), jnp.int32),
        pltpu.VMEM((NZ, 2, QD), jnp.int32),
        pltpu.VMEM((NZ, 2, QD), jnp.int32),
        pltpu.VMEM((NZ, 2, QD), F32),
        pltpu.VMEM((NZ, 2, QD), F32),
        pltpu.VMEM((NZ, 2, QD), F32),
        pltpu.VMEM((NZ, 2, QD), F32),
        pltpu.VMEM((NZ, 2, QD), F32),
        pltpu.VMEM((NZ, 2, QD), F32),
        pltpu.VMEM((HN, QD), F32),
        pltpu.VMEM((QD, HN), jnp.int32),
        pltpu.VMEM((QD, HN), F32),
        pltpu.VMEM((QD, HN), F32),
        pltpu.VMEM((QD, 1), F32),
        pltpu.VMEM((NZ, QD, D), F32),
        pltpu.VMEM((2 * QD, 2 * PD), BF16),
        pltpu.VMEM((2, 7, SUB, D), BF16),
        pltpu.VMEM((2, 7, SUB, D), BF16),
        pltpu.VMEM((NB, QD), BF16),
        pltpu.VMEM((2, NB, HD), F32),
        pltpu.VMEM((2, 2, 3, SLAB // 2, HD), BF16),
        pltpu.VMEM((2, 2, 3, SLAB // 2, HD), BF16),
        pltpu.VMEM((2, NY, IB, HD), F32),
        pltpu.VMEM((2, NY, IB, HD), BF16),
        pltpu.VMEM((2, NY, IB, HD), BF16),
        pltpu.VMEM((QD, D), F32),
        pltpu.VMEM((2, NZ * QD, D), BF16),
        pltpu.VMEM((PD, D), F32),
        pltpu.VMEM((PD, D), F32),
        pltpu.VMEM((PD, D), F32),
        pltpu.VMEM((PD, D), BF16),
        dma((4,)),
        dma((2, 7)),
        dma((2, 7)),
        dma((2, 7)),
        dma((2, 7)),
        dma((2, 2, 3)),
        dma((2, 2, 3)),
        dma((2, 2, 3)),
        dma((2, 2, 3)),
        dma((11,)),
        dma((11,)),
        pltpu.SemaphoreType.REGULAR,
        pltpu.SemaphoreType.REGULAR,
    ]
    shapes = (
        pltpu.VMEM((QD, D), BF16),
        pltpu.VMEM((IB, D), BF16),
        pltpu.VMEM((PD, D), BF16),
    )
    return pl.pallas_call(
        kernel,
        out_shape=shapes,
        in_specs=[hbm] * 4 + [vmem] * 4,
        out_specs=(vmem, vmem, vmem),
        scratch_shapes=scratch,
        compiler_params=pltpu.CompilerParams(
            collective_id=0, has_side_effects=True, vmem_limit_bytes=58 * 1024 * 1024
        ),
        cost_estimate=pl.CostEstimate(flops=9_000_000_000, bytes_accessed=6_000_000, transcendentals=100_000),
    )(
        queries, batch_hidden, pool_hidden, projection, hard_ids.T,
        query_group.reshape(1, QD), labels.reshape(1, QD), group_lists,
    )


def solution(mesh):
    return jax.shard_map(
        shards,
        mesh=mesh,
        in_specs=(
            P(("pa", "pb"), None),
            P(("pa", "pb"), None),
            P(("pa", "pb"), None),
            P(),
            P(("pa", "pb"), None),
            P(("pa", "pb")),
            P(("pa", "pb")),
            P(),
        ),
        out_specs=(P(("pa", "pb"), None), P(("pa", "pb"), None), P(("pa", "pb"), None)),
        check_vma=False,
    )
```
